32 devices in a mesh: fsdp: 4 (over z), seq: 2 (over x), head: 4 (over y, core).
Axes of the slice: x: 2, y: 2, z: 4, core: 2. Of those that a mesh axis runs over, the one named last changes fastest.
Arguments:
- queries: bfloat16 [2048, 4096], P(('fsdp', 'seq'), 'head'), may hold values from -6 to 6
- span_k: bfloat16 [2048, 512], P(('fsdp', 'seq'), 'head'), may hold values from -6 to 6
- span_v: bfloat16 [2048, 512], P(('fsdp', 'seq'), 'head'), may hold values from -6 to 6
- cache_k: bfloat16 [512, 128, 512], P(('fsdp', 'seq'), None, 'head'), may hold values from -6 to 6
- cache_v: bfloat16 [512, 128, 512], P(('fsdp', 'seq'), None, 'head'), may hold values from -6 to 6
- block_slot: int32 [512], replicated, may hold values from 0 to 511, as said below
- pattern: int32 [16, 48], P(('fsdp', 'seq')), may hold values from 0 to 511, as said below
- wo: bfloat16 [4096, 8192], P('head', 'fsdp'), may hold values from -6 to 6
Outputs:
- mixed: bfloat16 [2048, 8192], P(('fsdp', 'seq'))
The draws below stay inside these ranges and needn't reach their ends.
Inputs may be any that keep to these rules, and one draw needn't show every extreme that they name: `pattern`: each row lists 48 different blocks. Of the 96 entries in the rows of one index of fsdp and seq, all are different, at most 24 have a storage row block_slot between o * 64 and (o + 1) * 64 - 1 for any o, and exactly 24 do for some o. A permutation: block c is stored at row block_slot[c] of cache_k and cache_v.
All inputs are finite; a program needn't handle non-finite values.
Results may differ from the reference program's by a relative error of at most 0.0095.
Values may be sent and summed in bfloat16 or wider, within the bound.
No kernel may reach another device: no remote copies, remote signals or barrier semaphores. Data moves between devices by JAX's collectives and lax.ppermute only.
A program may use at most 128 MiB of HBM per device.

```python
import jax
import jax.numpy as jnp
from jax import lax

D = 8192
HD = 128
KVH = 4
GROUP = 8
BLK = 128
NLIST = 48
QB_DEV = 2
CB_DEV = 64
QH = 32
SEQ_DEVS = 8
QBLOCKS = 16
TOKENS = 2048
CACHE_BLOCKS = 512
CAP = 24
N_HEAD = 4


def draw_queries(key, part):
    shape = (TOKENS, QH * HD)
    values = jnp.clip(jax.random.normal(jax.random.fold_in(key, 1), shape), -6.0, 6.0)
    return values.astype(jnp.bfloat16)


def draw_cache_k(key, part):
    shape = (CACHE_BLOCKS, BLK, KVH * HD)
    values = jnp.clip(jax.random.normal(jax.random.fold_in(key, 4), shape), -6.0, 6.0)
    return values.astype(jnp.bfloat16)


def slot_layout(key):
    return jax.random.permutation(jax.random.fold_in(key, 11), CACHE_BLOCKS).astype(jnp.int32)


def draw_block_slot(key, part):
    return slot_layout(key)


def device_lists(device_key):
    requests = QB_DEV * NLIST
    pool = jnp.arange(SEQ_DEVS * CAP, dtype=jnp.int32) // CAP
    pool = jax.random.permutation(jax.random.fold_in(device_key, 1), pool)
    heavy = jax.random.randint(jax.random.fold_in(device_key, 2), (), 0, SEQ_DEVS).astype(jnp.int32)
    ranked = (pool == heavy).astype(jnp.int32) * (SEQ_DEVS * CAP) + jnp.arange(SEQ_DEVS * CAP, dtype=jnp.int32)
    taken = pool[jnp.argsort(ranked)][:requests - CAP]
    owners = jnp.concatenate([jnp.full((CAP,), heavy, jnp.int32), taken])
    position = jnp.arange(requests)
    earlier = (owners[None, :] == owners[:, None]) & (position[None, :] < position[:, None])
    ranking = jnp.sum(earlier.astype(jnp.int32), axis=1)
    offsets = jax.random.randint(jax.random.fold_in(device_key, 3), (SEQ_DEVS,), 0, CB_DEV).astype(jnp.int32)
    within = (offsets[owners] + ranking) % CB_DEV
    shuffle = jax.random.permutation(jax.random.fold_in(device_key, 4), requests)
    return (owners * CB_DEV + within)[shuffle]


def draw_pattern(key, part):
    base_key = jax.random.fold_in(key, 77)
    device_keys = jax.vmap(lambda device: jax.random.fold_in(base_key, device))(jnp.arange(SEQ_DEVS))
    slots = jax.vmap(device_lists)(device_keys)
    inverse = jnp.argsort(slot_layout(key)).astype(jnp.int32)
    return inverse[slots].reshape(QBLOCKS, NLIST).astype(jnp.int32)


def block_levels(stream_key, dims, split, low, largest):
    loudness, own = 1.0, jax.random.fold_in(stream_key, 6)
    for dim, blocks in split:
        steps = jnp.exp(jax.random.uniform(jax.random.fold_in(own, dim), (blocks,), jnp.float32, low / len(split), largest / len(split)))
        loudness = loudness * jnp.repeat(steps, dims[dim] // blocks).reshape([-1 if axis == dim else 1 for axis in range(len(dims))])
    return loudness


def noise(stream_key, dims, spread, reach, pieces=(), kind=jnp.bfloat16):
    values = spread * jax.random.normal(stream_key, dims, jnp.float32)
    if pieces:
        values = values * block_levels(stream_key, dims, pieces, -0.22, 0.18)
    return jnp.clip(values, -reach, reach).astype(kind)


def setup_inputs(seed: int = 0) -> dict:
    arg_keys = jax.random.split(jax.random.key(seed), 9)
    queries = draw_queries(jax.random.fold_in(arg_keys[8], 71), 0)
    span_k = noise(arg_keys[1], (TOKENS, KVH * HD), 1.0, 6.0, ((0, 8), (1, 4)))
    span_v = noise(arg_keys[2], (TOKENS, KVH * HD), 1.0, 6.0, ((0, 8), (1, 4)))
    cache_k = draw_cache_k(jax.random.fold_in(arg_keys[8], 71), 0)
    cache_v = noise(arg_keys[4], (CACHE_BLOCKS, BLK, KVH * HD), 1.0, 6.0, ((0, 8), (2, 4)))
    block_slot = draw_block_slot(jax.random.fold_in(arg_keys[8], 71), 0)
    pattern = draw_pattern(jax.random.fold_in(arg_keys[8], 71), 0)
    wo = noise(arg_keys[7], (QH * HD, D), 1.0, 6.0, ((0, 4), (1, 4)))
    return {"queries": queries, "span_k": span_k, "span_v": span_v, "cache_k": cache_k, "cache_v": cache_v, "block_slot": block_slot, "pattern": pattern, "wo": wo}


def attend_block(query_block, keys, values, present):
    length = keys.shape[0]
    block_len = query_block.shape[0]
    scores = jnp.einsum('tkgd,lkd->kgtl', query_block.astype(jnp.float32), keys.astype(jnp.float32)) / jnp.sqrt(jnp.float32(HD))
    column = jnp.arange(length)[None, :]
    row_ids = jnp.arange(block_len)[:, None]
    listed_end = length - 2 * block_len
    own_start = listed_end + block_len
    allowed = (column < listed_end) | (column >= listed_end) & (column < own_start) & present | (column >= own_start) & (column - own_start <= row_ids)
    scores = jnp.where(allowed, scores, -jnp.inf)
    top = lax.optimization_barrier(jnp.max(scores, axis=-1, keepdims=True))
    expo = jnp.exp(scores - top)
    probs_bf = (expo / lax.optimization_barrier(jnp.sum(expo, axis=-1, keepdims=True))).astype(jnp.bfloat16)
    output = jnp.einsum('kgtl,lkd->tkgd', probs_bf.astype(jnp.float32), values.astype(jnp.float32))
    return output.reshape(block_len, -1).astype(jnp.bfloat16)

def reference(queries, span_k, span_v, cache_k, cache_v, block_slot, pattern, wo):
    query_blocks = queries.reshape(QBLOCKS, BLK, KVH, GROUP, HD)
    own_k = span_k.reshape(QBLOCKS, BLK, KVH, HD)
    own_v = span_v.reshape(QBLOCKS, BLK, KVH, HD)

    def one_block(index):
        storage = block_slot[pattern[index]]
        listed_k = cache_k[storage].reshape(NLIST * BLK, KVH, HD)
        listed_v = cache_v[storage].reshape(NLIST * BLK, KVH, HD)
        before = jnp.maximum(index - 1, 0).astype(jnp.int32)
        keys = jnp.concatenate([listed_k, own_k[before], own_k[index]], axis=0)
        values = jnp.concatenate([listed_v, own_v[before], own_v[index]], axis=0)
        return attend_block(query_blocks[index], keys, values, index > 0)
    attended = lax.map(one_block, jnp.arange(QBLOCKS, dtype=jnp.int32)).reshape(TOKENS, QH * HD)
    group_cols = QH * HD // N_HEAD
    total = jnp.zeros((TOKENS, D), jnp.float32)
    for group_index in range(N_HEAD):
        lower = group_index * group_cols
        term = jnp.dot(attended[:, lower:lower + group_cols], wo[lower:lower + group_cols], preferred_element_type=jnp.float32).astype(jnp.bfloat16)
        term = lax.optimization_barrier(term)
        total = total + term.astype(jnp.float32)
    return total.astype(jnp.bfloat16)
```

```python
import functools
import math

import jax
import jax.numpy as jnp
from jax import lax
from jax.experimental import pallas as pl
from jax.experimental.pallas import tpu as pltpu
from jax.sharding import PartitionSpec as P

HD = 128
NEG = -1e30
F32 = jnp.float32
BF16 = jnp.bfloat16
VMEM_LIMIT = 48 * 1024 * 1024


def swap(value, axis, distance):
    count = lax.axis_size(axis)
    return lax.ppermute(value, axis, [(i, i ^ distance) for i in range(count)])


def stack_heads(q_ref, stacked):
    tokens = q_ref.shape[0]
    for h in range(q_ref.shape[1] // HD):
        stacked[h * tokens:(h + 1) * tokens, :] = q_ref[:, h * HD:(h + 1) * HD]


def write_partial(out_ref, acc, top):
    tokens = out_ref.shape[0]
    heads = (out_ref.shape[1] - HD) // HD
    lane = lax.broadcasted_iota(jnp.int32, (tokens, HD), 1)
    stats = jnp.zeros((tokens, HD), F32)
    for h in range(heads):
        rows = slice(h * tokens, (h + 1) * tokens)
        total = acc[rows, HD:]
        inverse = jnp.where(total > 0, 1.0 / total, 0.0)
        out_ref[:, h * HD:(h + 1) * HD] = (acc[rows, :HD] * inverse).astype(BF16)
        high = total.astype(BF16).astype(F32)
        stats = jnp.where(lane == h, top[rows, :].astype(F32), stats)
        stats = jnp.where(lane == heads + h, high, stats)
        stats = jnp.where(lane == 2 * heads + h, total - high, stats)
    out_ref[:, heads * HD:] = stats.astype(BF16)


def add_pair(acc, probs, values):
    ones = jnp.ones(values.shape, BF16)
    acc[...] += jnp.dot(probs, jnp.concatenate([values, ones], axis=1), preferred_element_type=F32)


def scaled_scores(stacked, keys):
    scores = lax.dot_general(stacked, keys, (((1,), (1,)), ((), ())), preferred_element_type=F32)
    return scores * (math.log2(math.e) / math.sqrt(HD))


def listed_kernel(blocks, table, *refs):
    q_refs, refs = refs[:blocks], refs[blocks:]
    k_hbm, v_hbm, refs = refs[0], refs[1], refs[2:]
    out_refs, refs = refs[:blocks], refs[blocks:]
    k_buf, v_buf, stacked, scores, acc, running, top, sems = refs
    block_len = k_hbm.shape[1]

    def pairs(j):
        return (table[j, 0] + 1) // 2

    def copies(j, i):
        slot, side = table[j, 1 + i], j % 2
        return (
            pltpu.make_async_copy(k_hbm.at[slot], k_buf.at[side, i], sems.at[side, 0]),
            pltpu.make_async_copy(v_hbm.at[slot], v_buf.at[side, i], sems.at[side, 1]),
        )

    def fetch(j):
        def one(i, carry):
            for copy in copies(j, i):
                copy.start()
            return carry
        lax.fori_loop(0, 2 * pairs(j), one, 0)

    def arrived(j):
        def one(i, carry):
            for copy in copies(j, i):
                copy.wait()
            return carry
        lax.fori_loop(0, 2 * pairs(j), one, 0)

    fetch(0)
    for j in range(blocks):
        side = j % 2
        if j + 1 < blocks:
            fetch(j + 1)
        stack_heads(q_refs[j], stacked)
        running[...] = jnp.full(running.shape, NEG, F32)
        acc[...] = jnp.zeros(acc.shape, F32)
        arrived(j)

        def first(i, carry):
            keys = k_buf[side, pl.ds(2 * i, 2)].reshape(2 * block_len, HD)
            found = scaled_scores(stacked[...], keys)
            bias = jnp.where(2 * i + 1 < table[j, 0], 0.0, NEG).astype(F32)
            one, two = found[:, :block_len], found[:, block_len:] + bias
            scores[i, :, :block_len] = one
            scores[i, :, block_len:] = two
            running[...] = jnp.maximum(running[...], jnp.maximum(one, two))
            return carry

        lax.fori_loop(0, pairs(j), first, 0)
        top[...] = jnp.broadcast_to(jnp.max(running[...], axis=1, keepdims=True), top.shape).astype(BF16)

        def second(i, carry):
            reference = top[...].astype(F32)
            probs = jnp.concatenate(
                [jnp.exp2(scores[i, :, :block_len] - reference), jnp.exp2(scores[i, :, block_len:] - reference)], axis=1
            ).astype(BF16)
            add_pair(acc, probs, v_buf[side, pl.ds(2 * i, 2)].reshape(2 * block_len, HD))
            return carry

        lax.fori_loop(0, pairs(j), second, 0)
        write_partial(out_refs[j], acc, top)


def attend_listed(table, queries, cache_k, cache_v):
    blocks = len(queries)
    tokens, columns = queries[0].shape
    rows = tokens * columns // HD
    block_len = cache_k.shape[1]
    capacity = table.shape[1] - 1
    vmem = pl.BlockSpec(memory_space=pltpu.VMEM)
    hbm = pl.BlockSpec(memory_space=pl.ANY)
    keys = blocks * block_len * 6
    return pl.pallas_call(
        functools.partial(listed_kernel, blocks),
        out_shape=[jax.ShapeDtypeStruct((tokens, columns + HD), BF16)] * blocks,
        in_specs=[pl.BlockSpec(memory_space=pltpu.SMEM)] + [vmem] * blocks + [hbm] * 2,
        out_specs=[vmem] * blocks,
        scratch_shapes=[
            pltpu.VMEM((2, capacity, block_len, HD), BF16),
            pltpu.VMEM((2, capacity, block_len, HD), BF16),
            pltpu.VMEM((rows, HD), BF16),
            pltpu.VMEM((capacity // 2, rows, 2 * block_len), F32),
            pltpu.VMEM((rows, 2 * HD), F32),
            pltpu.VMEM((rows, HD), F32),
            pltpu.VMEM((rows, HD), BF16),
            pltpu.SemaphoreType.DMA((2, 2)),
        ],
        compiler_params=pltpu.CompilerParams(vmem_limit_bytes=VMEM_LIMIT),
        cost_estimate=pl.CostEstimate(
            flops=4 * rows * keys * HD * 2, bytes_accessed=4 * keys * HD + 4 * blocks * rows * HD, transcendentals=rows * keys
        ),
    )(table, *queries, cache_k, cache_v)


def span_kernel(flag, q_ref, k0, k1, v0, v1, out_ref, stacked, acc, top):
    tokens = q_ref.shape[0]
    stack_heads(q_ref, stacked)
    keys = jnp.concatenate([k0[...], k1[...]], axis=0)
    found = scaled_scores(stacked[...], keys)
    row = lax.broadcasted_iota(jnp.int32, found.shape, 0) % tokens
    column = lax.broadcasted_iota(jnp.int32, found.shape, 1)
    behind = jnp.where(flag[0] > 0, tokens, 0)
    allowed = (column < behind) | ((column >= tokens) & (column - tokens <= row))
    found = jnp.where(allowed, found, NEG)
    top[...] = jnp.broadcast_to(jnp.max(found, axis=1, keepdims=True), top.shape).astype(BF16)
    reference = jnp.concatenate([top[...], top[...]], axis=1).astype(F32)
    acc[...] = jnp.zeros(acc.shape, F32)
    add_pair(acc, jnp.exp2(found - reference).astype(BF16), jnp.concatenate([v0[...], v1[...]], axis=0))
    write_partial(out_ref, acc, top)


def attend_span(flag, queries, k0, k1, v0, v1):
    tokens, columns = queries.shape
    rows = tokens * columns // HD
    vmem = pl.BlockSpec(memory_space=pltpu.VMEM)
    return pl.pallas_call(
        span_kernel,
        out_shape=jax.ShapeDtypeStruct((tokens, columns + HD), BF16),
        in_specs=[pl.BlockSpec(memory_space=pltpu.SMEM)] + [vmem] * 5,
        out_specs=vmem,
        scratch_shapes=[pltpu.VMEM((rows, HD), BF16), pltpu.VMEM((rows, 2 * HD), F32), pltpu.VMEM((rows, HD), BF16)],
        compiler_params=pltpu.CompilerParams(vmem_limit_bytes=VMEM_LIMIT),
        cost_estimate=pl.CostEstimate(flops=8 * rows * tokens * HD, bytes_accessed=6 * rows * HD, transcendentals=2 * rows * tokens),
    )(flag, queries, k0, k1, v0, v1)


def merge_kernel(count, final, *refs):
    parts, out_ref = refs[:count], refs[count]
    tokens = out_ref.shape[0]
    heads = (parts[0].shape[1] - HD) // HD
    stats = [part[:, heads * HD:].astype(F32) for part in parts]
    sums = [pltpu.roll(s, HD - heads, 1) + pltpu.roll(s, HD - 2 * heads, 1) for s in stats]
    top = functools.reduce(jnp.maximum, stats)
    weights = [jnp.exp2(s - top) * l for s, l in zip(stats, sums)]
    total = functools.reduce(jnp.add, weights)
    inverse = jnp.where(total > 0, 1.0 / total, 0.0)
    weights = [w * inverse for w in weights]
    for h in range(heads):
        columns = slice(h * HD, (h + 1) * HD)
        out_ref[:, columns] = functools.reduce(
            jnp.add, [w[:, h:h + 1] * part[:, columns].astype(F32) for w, part in zip(weights, parts)]
        ).astype(BF16)
    if not final:
        lane = lax.broadcasted_iota(jnp.int32, (tokens, HD), 1)
        high = total.astype(BF16).astype(F32)
        merged = jnp.where(lane < heads, top, pltpu.roll(high, heads, 1))
        merged = jnp.where(lane < 2 * heads, merged, pltpu.roll(total - high, 2 * heads, 1))
        out_ref[:, heads * HD:] = jnp.where(lane < 3 * heads, merged, 0.0).astype(BF16)


def merge(parts, final):
    tokens, columns = parts[0].shape
    vmem = pl.BlockSpec(memory_space=pltpu.VMEM)
    return pl.pallas_call(
        functools.partial(merge_kernel, len(parts), final),
        out_shape=jax.ShapeDtypeStruct((tokens, columns - HD if final else columns), BF16),
        in_specs=[vmem] * len(parts),
        out_specs=vmem,
        compiler_params=pltpu.CompilerParams(vmem_limit_bytes=VMEM_LIMIT),
        cost_estimate=pl.CostEstimate(
            flops=2 * len(parts) * tokens * columns, bytes_accessed=2 * (len(parts) + 1) * tokens * columns, transcendentals=0
        ),
    )(*parts)


def place_kernel(pieces, chunk, offsets, *refs):
    out_ref, buffer, sem = refs[-3:]
    n_z = refs[0].shape[0]
    tokens, width = refs[0].shape[1:]
    for j in range(pieces):
        for k in range(n_z):
            start = pl.multiple_of(offsets[j, k], width)
            buffer[:, pl.ds(start, width)] = refs[j][k]
    copy = pltpu.make_async_copy(buffer, out_ref.at[pl.ds(chunk * tokens, tokens)], sem)
    copy.start()
    copy.wait()


def place(offsets, pieces, chunk, chunks, before):
    n_z, tokens, width = pieces[0].shape
    columns = n_z * len(pieces) * width
    vmem = pl.BlockSpec(memory_space=pltpu.VMEM)
    hbm = pl.BlockSpec(memory_space=pl.ANY)
    held = [] if before is None else [before]
    return pl.pallas_call(
        functools.partial(place_kernel, len(pieces), chunk),
        out_shape=jax.ShapeDtypeStruct((chunks * tokens, columns), BF16),
        in_specs=[pl.BlockSpec(memory_space=pltpu.SMEM)] + [vmem] * len(pieces) + [hbm] * len(held),
        out_specs=hbm,
        scratch_shapes=[pltpu.VMEM((tokens, columns), BF16), pltpu.SemaphoreType.DMA],
        input_output_aliases={1 + len(pieces): 0} if held else {},
        compiler_params=pltpu.CompilerParams(vmem_limit_bytes=VMEM_LIMIT),
        cost_estimate=pl.CostEstimate(flops=0, bytes_accessed=4 * tokens * columns, transcendentals=0),
    )(offsets, *pieces, *held)


def body(queries, span_k, span_v, cache_k, cache_v, block_slot, pattern, wo):
    n_z, n_x, n_h = (lax.axis_size(a) for a in ("fsdp", "seq", "head"))
    z, x, me = (lax.axis_index(a) for a in ("fsdp", "seq", "head"))
    chunks, list_len = pattern.shape
    cb_local, block_len, _ = cache_k.shape
    index_here = z * n_x + x
    capacity = max(2, 2 * chunks * list_len // (n_z * n_x))
    capacity = min(capacity, list_len)
    capacity += capacity % 2

    slots = lax.all_gather(block_slot[pattern], ("fsdp", "seq"), axis=0, tiled=True)
    order = jnp.stack([
        ((z ^ k) * n_x + (x ^ s)) * chunks + c for c in range(chunks) for s in range(n_x) for k in range(n_z)
    ])
    slots = slots[order]
    within = slots - index_here * cb_local
    mine = (within >= 0) & (within < cb_local)
    rank = jnp.sum((mine[:, None, :] & jnp.tri(list_len, list_len, -1, dtype=bool)[None]).astype(jnp.int32), axis=2)
    place_of = jnp.where(mine, rank, -1)
    compact = jnp.sum(jnp.where(place_of[:, None, :] == jnp.arange(capacity)[None, :, None], within[:, None, :], 0), axis=2)
    table = jnp.concatenate([jnp.sum(mine.astype(jnp.int32), axis=1, keepdims=True), compact], axis=1)
    table = table.reshape(chunks, n_x, n_z, capacity + 1)

    n_index = n_z * n_x
    prior = lax.ppermute(
        jnp.concatenate([span_k[-block_len:], span_v[-block_len:]], axis=1),
        ("fsdp", "seq"), [(i, i + 1) for i in range(n_index - 1)],
    )

    quarter = wo.shape[1] // n_h
    columns_of = [lax.dynamic_slice_in_dim(wo, (me ^ j) * quarter, quarter, axis=1) for j in range(n_h)]
    offsets = jnp.stack([jnp.stack([(z ^ k) * wo.shape[1] + (me ^ j) * quarter for k in range(n_z)]) for j in range(n_h)])

    mixed = None
    for c in range(chunks):
        rows = slice(c * block_len, (c + 1) * block_len)
        own = queries[rows]
        by_z = [own] + [swap(own, "fsdp", k) for k in range(1, n_z)]
        if c == 0:
            k0, v0 = prior[:, :HD], prior[:, HD:]
        else:
            before = slice((c - 1) * block_len, c * block_len)
            k0, v0 = span_k[before], span_v[before]
        flag = (index_here * chunks + c > 0).astype(jnp.int32).reshape(1)
        span_part = attend_span(flag, own, k0, span_k[rows], v0, span_v[rows])
        gathered = [[swap(q, "seq", s) for q in by_z] for s in range(1, n_x)]
        away = [attend_listed(table[c, s], gathered[s - 1], cache_k, cache_v) for s in range(1, n_x)]
        here = attend_listed(table[c, 0], by_z, cache_k, cache_v)
        parts = [[here[k]] + [swap(away[s - 1][k], "seq", s) for s in range(1, n_x)] for k in range(n_z)]
        returned = [swap(merge(parts[k], False), "fsdp", k) for k in range(1, n_z)]
        attended = merge(returned + parts[0] + [span_part], True)

        all_z = jnp.concatenate([attended] + [swap(attended, "fsdp", k) for k in range(1, n_z)], axis=0)
        terms = [jnp.dot(all_z, w, preferred_element_type=F32).astype(BF16) for w in columns_of]
        distance = 1
        while distance < n_h:
            kept = [j for j in range(0, n_h, 2 * distance)]
            got = swap(jnp.concatenate([terms[j + distance] for j in kept], axis=1), "head", distance)
            for at, j in enumerate(kept):
                terms[j] = (terms[j].astype(F32) + got[:, at * quarter:(at + 1) * quarter].astype(F32)).astype(BF16)
            distance *= 2
        summed = terms[0].reshape(n_z, block_len, quarter)
        pieces = [jnp.stack([summed[0]] + [swap(summed[k], "fsdp", k) for k in range(1, n_z)])]
        while distance > 1:
            distance //= 2
            got = swap(jnp.stack(pieces), "head", distance)
            pieces = pieces + [got[i] for i in range(len(pieces))]
        step, names = n_h, [0]
        while step > 1:
            step //= 2
            names = names + [i ^ step for i in names]
        pieces = [pieces[names.index(j)] for j in range(n_h)]
        mixed = place(offsets, pieces, c, chunks, mixed)
    return mixed


def solution(mesh):
    return jax.shard_map(
        body,
        mesh=mesh,
        in_specs=(
            P(("fsdp", "seq"), "head"),
            P(("fsdp", "seq"), "head"),
            P(("fsdp", "seq"), "head"),
            P(("fsdp", "seq"), None, "head"),
            P(("fsdp", "seq"), None, "head"),
            P(),
            P(("fsdp", "seq"), None),
            P("head", "fsdp"),
        ),
        out_specs=P(("fsdp", "seq"), None),
        check_vma=False,
    )
```

```python
import functools
import math

import jax
import jax.numpy as jnp
from jax import lax
from jax.experimental import pallas as pl
from jax.experimental.pallas import tpu as pltpu
from jax.sharding import PartitionSpec as P

HD = 128
NEG = -1e30
STATS = 16
F32 = jnp.float32
BF16 = jnp.bfloat16
VMEM_LIMIT = 48 * 1024 * 1024


def swap(value, axis, distance):
    count = lax.axis_size(axis)
    return lax.ppermute(value, axis, [(i, i ^ distance) for i in range(count)])


def stack_heads(q_ref, stacked):
    tokens = q_ref.shape[0]
    for h in range(q_ref.shape[1] // HD):
        rows = slice(h * tokens, (h + 1) * tokens)
        scaled = q_ref[:, h * HD:(h + 1) * HD].astype(F32) * (math.log2(math.e) / math.sqrt(HD))
        high = scaled.astype(BF16)
        stacked[rows, :HD] = high
        stacked[rows, HD:] = (scaled - high.astype(F32)).astype(BF16)


def scores_of(keys, stacked):
    twice = jnp.concatenate([keys, keys], axis=1)
    return lax.dot_general(twice, stacked[...], (((1,), (1,)), ((), ())), preferred_element_type=F32)


def weigh(values, probs):
    return lax.dot_general(values, probs.astype(BF16), (((0,), (0,)), ((), ())), preferred_element_type=F32)


def in_eights(array):
    return array.reshape(array.shape[0] // 8, 8, array.shape[1])


def write_partial(out_ref, acc, total, top):
    inverse = jnp.where(total > 0, 1.0 / total, 0.0)
    out_ref[:HD] = (acc[...] * inverse).astype(BF16)
    write_stats(out_ref, total, top)


def write_stats(out_ref, total, top):
    high = total.astype(BF16).astype(F32)
    row = lax.broadcasted_iota(jnp.int32, (STATS, out_ref.shape[1]), 0)
    stats = jnp.where(row == 0, top, jnp.where(row == 1, high, jnp.where(row == 2, total - high, 0.0)))
    out_ref[HD:] = stats.astype(BF16)


def listed_kernel(blocks, table, *refs):
    q_refs, refs = refs[:blocks], refs[blocks:]
    k_ref, v_ref, refs = refs[0], refs[1], refs[2:]
    out_refs, (stacked, scores, acc) = refs[:blocks], refs[blocks:]
    block_len = k_ref.shape[1]
    columns = stacked.shape[0]
    for j in range(blocks):
        count = table[j, 0]
        stack_heads(q_refs[j], stacked)
        acc[...] = jnp.zeros(acc.shape, F32)

        def first(group, base, i, running):
            at = base + group * i
            keys = jnp.concatenate([k_ref[table[j, 1 + at + g]] for g in range(group)], axis=0)
            found = scores_of(keys, stacked)
            for g in range(group):
                part = found[g * block_len:(g + 1) * block_len]
                if g:
                    part = part + jnp.where(at + g < count, 0.0, NEG).astype(F32)
                scores[at + g] = part
                running = jnp.maximum(running, jnp.max(in_eights(part), axis=0))
            return running

        def second(group, base, i, total):
            at = base + group * i
            found = scores[pl.ds(at, group)].reshape(group * block_len // 8, 8, columns)
            probs = jnp.exp2(found - top_eight[None])
            values = jnp.concatenate([v_ref[table[j, 1 + at + g]] for g in range(group)], axis=0)
            acc[...] += weigh(values, probs.reshape(group * block_len, columns))
            return total + jnp.sum(probs, axis=0)

        def over(step, carry):
            fours = (count + 1) // 4
            carry = lax.fori_loop(0, fours, functools.partial(step, 4, 0), carry)
            rest = (jnp.maximum(count - 4 * fours, 0) + 1) // 2
            return lax.fori_loop(0, rest, functools.partial(step, 2, 4 * fours), carry)

        running = over(first, jnp.full((8, columns), NEG, F32))
        top = jnp.max(running, axis=0, keepdims=True).astype(BF16).astype(F32)
        top_eight = jnp.broadcast_to(top, (8, columns))
        total = jnp.sum(over(second, jnp.zeros((8, columns), F32)), axis=0, keepdims=True)
        write_partial(out_refs[j], acc, total, top)


def attend_listed(table, queries, cache_k, cache_v):
    blocks = len(queries)
    tokens, width = queries[0].shape
    columns = tokens * width // HD
    block_len = cache_k.shape[1]
    vmem = pl.BlockSpec(memory_space=pltpu.VMEM)
    keys = blocks * block_len * 6
    return pl.pallas_call(
        functools.partial(listed_kernel, blocks),
        out_shape=[jax.ShapeDtypeStruct((HD + STATS, columns), BF16)] * blocks,
        in_specs=[pl.BlockSpec(memory_space=pltpu.SMEM)] + [vmem] * (blocks + 2),
        out_specs=[vmem] * blocks,
        scratch_shapes=[
            pltpu.VMEM((columns, 2 * HD), BF16),
            pltpu.VMEM((table.shape[1] - 1, block_len, columns), F32),
            pltpu.VMEM((HD, columns), F32),
        ],
        compiler_params=pltpu.CompilerParams(vmem_limit_bytes=VMEM_LIMIT),
        cost_estimate=pl.CostEstimate(
            flops=8 * columns * keys * HD, bytes_accessed=4 * cache_k.size, transcendentals=columns * keys
        ),
    )(table, *queries, cache_k, cache_v)


def span_kernel(flag, q_ref, k0, k1, v0, v1, out_ref, stacked, acc):
    tokens = q_ref.shape[0]
    stack_heads(q_ref, stacked)
    found = scores_of(jnp.concatenate([k0[...], k1[...]], axis=0), stacked)
    key = lax.broadcasted_iota(jnp.int32, found.shape, 0)
    token = lax.broadcasted_iota(jnp.int32, found.shape, 1) % tokens
    behind = jnp.where(flag[0] > 0, tokens, 0)
    found = jnp.where((key < behind) | ((key >= tokens) & (key - tokens <= token)), found, NEG)
    top = jnp.max(found, axis=0, keepdims=True).astype(BF16).astype(F32)
    probs = jnp.exp2(found - top)
    acc[...] = weigh(jnp.concatenate([v0[...], v1[...]], axis=0), probs)
    write_partial(out_ref, acc, jnp.sum(probs, axis=0, keepdims=True), top)


def attend_span(flag, queries, k0, k1, v0, v1):
    tokens, width = queries.shape
    columns = tokens * width // HD
    vmem = pl.BlockSpec(memory_space=pltpu.VMEM)
    return pl.pallas_call(
        span_kernel,
        out_shape=jax.ShapeDtypeStruct((HD + STATS, columns), BF16),
        in_specs=[pl.BlockSpec(memory_space=pltpu.SMEM)] + [vmem] * 5,
        out_specs=vmem,
        scratch_shapes=[pltpu.VMEM((columns, 2 * HD), BF16), pltpu.VMEM((HD, columns), F32)],
        compiler_params=pltpu.CompilerParams(vmem_limit_bytes=VMEM_LIMIT),
        cost_estimate=pl.CostEstimate(flops=8 * columns * tokens * HD, bytes_accessed=6 * columns * HD, transcendentals=2 * columns * tokens),
    )(flag, queries, k0, k1, v0, v1)


def merge_kernel(count, final, *refs):
    parts, out_ref = refs[:count], refs[count]
    stats = [part[HD:].astype(F32) for part in parts]
    tops = [s[0:1] for s in stats]
    top = functools.reduce(jnp.maximum, tops)
    weights = [jnp.exp2(t - top) * (s[1:2] + s[2:3]) for t, s in zip(tops, stats)]
    total = functools.reduce(jnp.add, weights)
    inverse = jnp.where(total > 0, 1.0 / total, 0.0)
    weights = [w * inverse for w in weights]
    tokens = out_ref.shape[0] if final else HD
    for lower in range(0, parts[0].shape[1], tokens):
        columns = slice(lower, lower + tokens)
        joined = functools.reduce(jnp.add, [w[:, columns] * part[:HD, columns].astype(F32) for w, part in zip(weights, parts)])
        if final:
            h = lower // tokens
            out_ref[:, h * HD:(h + 1) * HD] = joined.T.astype(BF16)
        else:
            out_ref[:HD, columns] = joined.astype(BF16)
    if not final:
        write_stats(out_ref, total, top)


def merge(parts, tokens=None):
    rows, columns = parts[0].shape
    vmem = pl.BlockSpec(memory_space=pltpu.VMEM)
    shape = (tokens, columns * HD // tokens) if tokens else (rows, columns)
    return pl.pallas_call(
        functools.partial(merge_kernel, len(parts), tokens is not None),
        out_shape=jax.ShapeDtypeStruct(shape, BF16),
        in_specs=[vmem] * len(parts),
        out_specs=vmem,
        compiler_params=pltpu.CompilerParams(vmem_limit_bytes=VMEM_LIMIT),
        cost_estimate=pl.CostEstimate(
            flops=2 * len(parts) * rows * columns, bytes_accessed=2 * (len(parts) + 1) * rows * columns, transcendentals=0
        ),
    )(*parts)


def project_kernel(count, picks, offsets, *refs):
    parts, wo_ref, out_ref, stacked = refs[:count], refs[count], refs[count + 1], refs[count + 2]
    tokens = parts[0].shape[0]
    width = out_ref.shape[1] // len(picks)
    for k, part in enumerate(parts):
        stacked[k * tokens:(k + 1) * tokens] = part[...]
    for at, j in enumerate(picks):
        start = pl.multiple_of(offsets[j], width)
        out_ref[:, at * width:(at + 1) * width] = jnp.dot(
            stacked[...], wo_ref[:, pl.ds(start, width)], preferred_element_type=F32
        ).astype(BF16)


def project(offsets, parts, wo, picks):
    tokens, depth = parts[0].shape
    width = wo.shape[1] // offsets.shape[0] * len(picks)
    rows = len(parts) * tokens
    vmem = pl.BlockSpec(memory_space=pltpu.VMEM)
    return pl.pallas_call(
        functools.partial(project_kernel, len(parts), tuple(picks)),
        out_shape=jax.ShapeDtypeStruct((rows, width), BF16),
        in_specs=[pl.BlockSpec(memory_space=pltpu.SMEM)] + [vmem] * (len(parts) + 1),
        out_specs=vmem,
        scratch_shapes=[pltpu.VMEM((rows, depth), BF16)],
        compiler_params=pltpu.CompilerParams(vmem_limit_bytes=VMEM_LIMIT),
        cost_estimate=pl.CostEstimate(
            flops=2 * rows * depth * width, bytes_accessed=2 * (rows * (depth + width) + depth * width), transcendentals=0
        ),
    )(offsets, *parts, wo)


def place_kernel(pieces, n_z, chunk, offsets, *refs):
    out_ref, buffer, sem = refs[-3:]
    tokens = refs[0].shape[0] // n_z
    width = refs[0].shape[1]
    for j in range(pieces):
        for k in range(n_z):
            start = pl.multiple_of(offsets[j, k], width)
            buffer[:, pl.ds(start, width)] = refs[j][k * tokens:(k + 1) * tokens]
    copy = pltpu.make_async_copy(buffer, out_ref.at[pl.ds(chunk * tokens, tokens)], sem)
    copy.start()
    copy.wait()


def place(offsets, pieces, chunk, chunks, before):
    n_z = offsets.shape[1]
    rows, width = pieces[0].shape
    tokens = rows // n_z
    columns = n_z * len(pieces) * width
    vmem = pl.BlockSpec(memory_space=pltpu.VMEM)
    hbm = pl.BlockSpec(memory_space=pl.ANY)
    held = [] if before is None else [before]
    return pl.pallas_call(
        functools.partial(place_kernel, len(pieces), n_z, chunk),
        out_shape=jax.ShapeDtypeStruct((chunks * tokens, columns), BF16),
        in_specs=[pl.BlockSpec(memory_space=pltpu.SMEM)] + [vmem] * len(pieces) + [hbm] * len(held),
        out_specs=hbm,
        scratch_shapes=[pltpu.VMEM((tokens, columns), BF16), pltpu.SemaphoreType.DMA],
        input_output_aliases={1 + len(pieces): 0} if held else {},
        compiler_params=pltpu.CompilerParams(vmem_limit_bytes=VMEM_LIMIT),
        cost_estimate=pl.CostEstimate(flops=0, bytes_accessed=4 * tokens * columns, transcendentals=0),
    )(offsets, *pieces, *held)


def body(queries, span_k, span_v, cache_k, cache_v, block_slot, pattern, wo):
    n_z, n_x, n_h = (lax.axis_size(a) for a in ("fsdp", "seq", "head"))
    z, x, me = (lax.axis_index(a) for a in ("fsdp", "seq", "head"))
    chunks, list_len = pattern.shape
    cb_local, block_len, _ = cache_k.shape
    index_here = z * n_x + x
    capacity = min(max(2, 2 * chunks * list_len // (n_z * n_x)), list_len)
    capacity = -(-capacity // 4) * 4

    slots = block_slot[pattern]
    slots = jnp.stack([slots] + [swap(slots, "fsdp", k) for k in range(1, n_z)])
    slots = jnp.stack([slots] + [swap(slots, "seq", s) for s in range(1, n_x)])
    within = slots - index_here * cb_local
    mine = (within >= 0) & (within < cb_local)
    before = jnp.tri(list_len, list_len, -1, dtype=bool)
    rank = jnp.sum((mine[..., None, :] & before).astype(jnp.int32), axis=-1)
    rank = jnp.where(mine, rank, -1)
    chosen = rank[..., None, :] == jnp.arange(capacity)[:, None]
    compact = jnp.sum(jnp.where(chosen, within[..., None, :], 0), axis=-1)
    table = jnp.concatenate([jnp.sum(mine.astype(jnp.int32), axis=-1, keepdims=True), compact], axis=-1)

    prior = lax.ppermute(
        jnp.concatenate([span_k[-block_len:], span_v[-block_len:]], axis=1),
        ("fsdp", "seq"), [(i, i + 1) for i in range(n_z * n_x - 1)],
    )

    quarter = wo.shape[1] // n_h
    picked = jnp.stack([(me ^ j) * quarter for j in range(n_h)])
    offsets = jnp.stack([jnp.stack([(z ^ k) * wo.shape[1] + (me ^ j) * quarter for k in range(n_z)]) for j in range(n_h)])

    mixed = None
    for c in range(chunks):
        rows = slice(c * block_len, (c + 1) * block_len)
        own = queries[rows]
        by_z = [own] + [swap(own, "fsdp", k) for k in range(1, n_z)]
        if c == 0:
            k0, v0 = prior[:, :HD], prior[:, HD:]
        else:
            earlier = slice((c - 1) * block_len, c * block_len)
            k0, v0 = span_k[earlier], span_v[earlier]
        flag = (index_here * chunks + c > 0).astype(jnp.int32).reshape(1)
        span_part = attend_span(flag, own, k0, span_k[rows], v0, span_v[rows])
        gathered = [[swap(q, "seq", s) for q in by_z] for s in range(1, n_x)]
        away = [attend_listed(table[s, :, c], gathered[s - 1], cache_k, cache_v) for s in range(1, n_x)]
        here = attend_listed(table[0, :, c], by_z, cache_k, cache_v)
        parts = [[here[k]] + [swap(away[s - 1][k], "seq", s) for s in range(1, n_x)] for k in range(n_z)]
        returned = [swap(merge(parts[k]), "fsdp", k) for k in range(1, n_z)]
        attended = merge(returned + parts[0] + [span_part], block_len)

        all_z = [attended] + [swap(attended, "fsdp", k) for k in range(1, n_z)]
        kept = [j for j in range(n_h) if j % 2 == 0] if n_h > 1 else [0]
        sent = [j ^ 1 for j in kept] if n_h > 1 else []
        if sent:
            got = swap(project(picked, all_z, wo, sent), "head", 1)
            held = project(picked, all_z, wo, kept).astype(F32) + got.astype(F32)
        else:
            held = project(picked, all_z, wo, kept).astype(F32)
        distance = 2
        while distance < n_h:
            stay = [i for i, j in enumerate(kept) if j % (2 * distance) == 0]
            go = [kept.index(kept[i] ^ distance) for i in stay]
            cut = lambda ids: jnp.concatenate([held[:, i * quarter:(i + 1) * quarter] for i in ids], axis=1)
            got = swap(cut(go).astype(BF16), "head", distance)
            held = cut(stay) + got.astype(F32)
            kept = [kept[i] for i in stay]
            distance *= 2
        summed = held.astype(BF16)
        pieces = {0: jnp.concatenate(
            [summed[:block_len]]
            + [swap(summed[k * block_len:(k + 1) * block_len], "fsdp", k) for k in range(1, n_z)], axis=0
        )}
        while distance > 1:
            distance //= 2
            for j in list(pieces):
                pieces[j ^ distance] = swap(pieces[j], "head", distance)
        mixed = place(offsets, [pieces[j] for j in range(n_h)], c, chunks, mixed)
    return mixed


def solution(mesh):
    return jax.shard_map(
        body,
        mesh=mesh,
        in_specs=(
            P(("fsdp", "seq"), "head"),
            P(("fsdp", "seq"), "head"),
            P(("fsdp", "seq"), "head"),
            P(("fsdp", "seq"), None, "head"),
            P(("fsdp", "seq"), None, "head"),
            P(),
            P(("fsdp", "seq"), None),
            P("head", "fsdp"),
        ),
        out_specs=P(("fsdp", "seq"), None),
        check_vma=False,
    )
```

```python
import functools
import math

import jax
import jax.numpy as jnp
from jax import lax
from jax.experimental import pallas as pl
from jax.experimental.pallas import tpu as pltpu
from jax.sharding import PartitionSpec as P

HD = 128
NEG = -1e30
STATS = 16
F32 = jnp.float32
BF16 = jnp.bfloat16
MIB = 1024 * 1024


def swap(value, axis, distance):
    count = lax.axis_size(axis)
    return lax.ppermute(value, axis, [(i, i ^ distance) for i in range(count)])


def stack_heads(q_ref, stacked):
    tokens = q_ref.shape[0]
    for h in range(q_ref.shape[1] // HD):
        rows = slice(h * tokens, (h + 1) * tokens)
        scaled = q_ref[:, h * HD:(h + 1) * HD].astype(F32) * (math.log2(math.e) / math.sqrt(HD))
        high = scaled.astype(BF16)
        stacked[rows, :HD] = high
        stacked[rows, HD:] = (scaled - high.astype(F32)).astype(BF16)


def scores_of(keys, stacked):
    twice = jnp.concatenate([keys, keys], axis=1)
    return lax.dot_general(twice, stacked[...], (((1,), (1,)), ((), ())), preferred_element_type=F32)


def weigh(values, probs):
    return lax.dot_general(values, probs.astype(BF16), (((0,), (0,)), ((), ())), preferred_element_type=F32)


def in_eights(array):
    return array.reshape(array.shape[0] // 8, 8, array.shape[1])


def write_partial(out_ref, acc, total, top):
    inverse = jnp.where(total > 0, 1.0 / total, 0.0)
    out_ref[:HD] = (acc[...] * inverse).astype(BF16)
    write_stats(out_ref, total, top)


def write_stats(out_ref, total, top):
    high = total.astype(BF16).astype(F32)
    row = lax.broadcasted_iota(jnp.int32, (STATS, out_ref.shape[1]), 0)
    stats = jnp.where(row == 0, top, jnp.where(row == 1, high, jnp.where(row == 2, total - high, 0.0)))
    out_ref[HD:] = stats.astype(BF16)


def listed_kernel(blocks, table, *refs):
    q_refs, refs = refs[:blocks], refs[blocks:]
    k_ref, v_ref, refs = refs[0], refs[1], refs[3:]
    out_refs, (stacked, scores, acc) = refs[:blocks], refs[blocks:]
    block_len = k_ref.shape[1]
    columns = stacked.shape[0]
    for j in range(blocks):
        count = table[j, 0]
        stack_heads(q_refs[j], stacked)
        acc[...] = jnp.zeros(acc.shape, F32)

        def first(group, base, i, running):
            at = base + group * i
            keys = jnp.concatenate([k_ref[table[j, 1 + at + g]] for g in range(group)], axis=0)
            found = scores_of(keys, stacked)
            for g in range(group):
                part = found[g * block_len:(g + 1) * block_len]
                if g:
                    part = part + jnp.where(at + g < count, 0.0, NEG).astype(F32)
                scores[at + g] = part
                running = jnp.maximum(running, jnp.max(in_eights(part), axis=0))
            return running

        def second(group, base, i, total):
            at = base + group * i
            found = scores[pl.ds(at, group)].reshape(group * block_len // 8, 8, columns)
            probs = jnp.exp2(found - top_eight[None])
            values = jnp.concatenate([v_ref[table[j, 1 + at + g]] for g in range(group)], axis=0)
            acc[...] += weigh(values, probs.reshape(group * block_len, columns))
            return total + jnp.sum(probs, axis=0)

        def over(step, carry):
            fours = (count + 1) // 4
            carry = lax.fori_loop(0, fours, functools.partial(step, 4, 0), carry)
            rest = (jnp.maximum(count - 4 * fours, 0) + 1) // 2
            return lax.fori_loop(0, rest, functools.partial(step, 2, 4 * fours), carry)

        running = over(first, jnp.full((8, columns), NEG, F32))
        top = jnp.max(running, axis=0, keepdims=True).astype(BF16).astype(F32)
        top_eight = jnp.broadcast_to(top, (8, columns))
        total = jnp.sum(over(second, jnp.zeros((8, columns), F32)), axis=0, keepdims=True)
        write_partial(out_refs[j], acc, total, top)


def attend_listed(after, table, queries, cache_k, cache_v):
    blocks = len(queries)
    tokens, width = queries[0].shape
    columns = tokens * width // HD
    block_len = cache_k.shape[1]
    vmem = pl.BlockSpec(memory_space=pltpu.VMEM)
    keys = blocks * block_len * 6
    return pl.pallas_call(
        functools.partial(listed_kernel, blocks),
        out_shape=[jax.ShapeDtypeStruct((HD + STATS, columns), BF16)] * blocks,
        in_specs=[pl.BlockSpec(memory_space=pltpu.SMEM)] + [vmem] * (blocks + 2) + [pl.BlockSpec(memory_space=pl.ANY)],
        out_specs=[vmem] * blocks,
        scratch_shapes=[
            pltpu.VMEM((columns, 2 * HD), BF16),
            pltpu.VMEM((table.shape[1] - 1, block_len, columns), F32),
            pltpu.VMEM((HD, columns), F32),
        ],
        compiler_params=pltpu.CompilerParams(vmem_limit_bytes=24 * MIB),
        cost_estimate=pl.CostEstimate(
            flops=8 * columns * keys * HD, bytes_accessed=4 * cache_k.size, transcendentals=columns * keys
        ),
    )(table, *queries, cache_k, cache_v, after)


def span_kernel(flag, q_ref, k0, k1, v0, v1, after, out_ref, stacked, acc):
    tokens = q_ref.shape[0]
    stack_heads(q_ref, stacked)
    found = scores_of(jnp.concatenate([k0[...], k1[...]], axis=0), stacked)
    key = lax.broadcasted_iota(jnp.int32, found.shape, 0)
    token = lax.broadcasted_iota(jnp.int32, found.shape, 1) % tokens
    behind = jnp.where(flag[0] > 0, tokens, 0)
    found = jnp.where((key < behind) | ((key >= tokens) & (key - tokens <= token)), found, NEG)
    top = jnp.max(found, axis=0, keepdims=True).astype(BF16).astype(F32)
    probs = jnp.exp2(found - top)
    acc[...] = weigh(jnp.concatenate([v0[...], v1[...]], axis=0), probs)
    write_partial(out_ref, acc, jnp.sum(probs, axis=0, keepdims=True), top)


def attend_span(after, flag, queries, k0, k1, v0, v1):
    tokens, width = queries.shape
    columns = tokens * width // HD
    vmem = pl.BlockSpec(memory_space=pltpu.VMEM)
    return pl.pallas_call(
        span_kernel,
        out_shape=jax.ShapeDtypeStruct((HD + STATS, columns), BF16),
        in_specs=[pl.BlockSpec(memory_space=pltpu.SMEM)] + [vmem] * 5 + [pl.BlockSpec(memory_space=pl.ANY)],
        out_specs=vmem,
        scratch_shapes=[pltpu.VMEM((columns, 2 * HD), BF16), pltpu.VMEM((HD, columns), F32)],
        compiler_params=pltpu.CompilerParams(vmem_limit_bytes=8 * MIB),
        cost_estimate=pl.CostEstimate(flops=8 * columns * tokens * HD, bytes_accessed=6 * columns * HD, transcendentals=2 * columns * tokens),
    )(flag, queries, k0, k1, v0, v1, after)


def merge_kernel(count, final, *refs):
    parts, out_ref = refs[:count], refs[count + 1]
    stats = [part[HD:].astype(F32) for part in parts]
    tops = [s[0:1] for s in stats]
    top = functools.reduce(jnp.maximum, tops)
    weights = [jnp.exp2(t - top) * (s[1:2] + s[2:3]) for t, s in zip(tops, stats)]
    total = functools.reduce(jnp.add, weights)
    inverse = jnp.where(total > 0, 1.0 / total, 0.0)
    weights = [w * inverse for w in weights]
    tokens = out_ref.shape[0] if final else HD
    for lower in range(0, parts[0].shape[1], tokens):
        columns = slice(lower, lower + tokens)
        joined = functools.reduce(jnp.add, [w[:, columns] * part[:HD, columns].astype(F32) for w, part in zip(weights, parts)])
        if final:
            h = lower // tokens
            out_ref[:, h * HD:(h + 1) * HD] = joined.T.astype(BF16)
        else:
            out_ref[:HD, columns] = joined.astype(BF16)
    if not final:
        write_stats(out_ref, total, top)


def merge(after, parts, tokens=None):
    rows, columns = parts[0].shape
    vmem = pl.BlockSpec(memory_space=pltpu.VMEM)
    shape = (tokens, columns * HD // tokens) if tokens else (rows, columns)
    return pl.pallas_call(
        functools.partial(merge_kernel, len(parts), tokens is not None),
        out_shape=jax.ShapeDtypeStruct(shape, BF16),
        in_specs=[vmem] * len(parts) + [pl.BlockSpec(memory_space=pl.ANY)],
        out_specs=vmem,
        compiler_params=pltpu.CompilerParams(vmem_limit_bytes=8 * MIB),
        cost_estimate=pl.CostEstimate(
            flops=2 * len(parts) * rows * columns, bytes_accessed=2 * (len(parts) + 1) * rows * columns, transcendentals=0
        ),
    )(*parts, after)


def project_kernel(count, picks, offsets, *refs):
    parts, wo_ref, out_ref, stacked = refs[:count], refs[count], refs[count + 2], refs[count + 3]
    tokens = parts[0].shape[0]
    width = out_ref.shape[1] // len(picks)
    for k, part in enumerate(parts):
        stacked[k * tokens:(k + 1) * tokens] = part[...]
    for at, j in enumerate(picks):
        start = pl.multiple_of(offsets[j], width)
        out_ref[:, at * width:(at + 1) * width] = jnp.dot(
            stacked[...], wo_ref[:, pl.ds(start, width)], preferred_element_type=F32
        ).astype(BF16)


def project(after, offsets, parts, wo, picks):
    tokens, depth = parts[0].shape
    width = wo.shape[1] // offsets.shape[0] * len(picks)
    rows = len(parts) * tokens
    vmem = pl.BlockSpec(memory_space=pltpu.VMEM)
    return pl.pallas_call(
        functools.partial(project_kernel, len(parts), tuple(picks)),
        out_shape=jax.ShapeDtypeStruct((rows, width), BF16),
        in_specs=[pl.BlockSpec(memory_space=pltpu.SMEM)] + [vmem] * (len(parts) + 1) + [pl.BlockSpec(memory_space=pl.ANY)],
        out_specs=vmem,
        scratch_shapes=[pltpu.VMEM((rows, depth), BF16)],
        compiler_params=pltpu.CompilerParams(vmem_limit_bytes=12 * MIB),
        cost_estimate=pl.CostEstimate(
            flops=2 * rows * depth * width, bytes_accessed=2 * (rows * (depth + width) + depth * width), transcendentals=0
        ),
    )(offsets, *parts, wo, after)


def place_kernel(pieces, n_z, chunk, offsets, *refs):
    out_ref, buffer, sem = refs[-3:]
    tokens = refs[0].shape[0] // n_z
    width = refs[0].shape[1]
    for j in range(pieces):
        for k in range(n_z):
            start = pl.multiple_of(offsets[j, k], width)
            buffer[:, pl.ds(start, width)] = refs[j][k * tokens:(k + 1) * tokens]
    copy = pltpu.make_async_copy(buffer, out_ref.at[pl.ds(chunk * tokens, tokens)], sem)
    copy.start()
    copy.wait()


def place(offsets, pieces, chunk, chunks, before):
    n_z = offsets.shape[1]
    rows, width = pieces[0].shape
    tokens = rows // n_z
    columns = n_z * len(pieces) * width
    vmem = pl.BlockSpec(memory_space=pltpu.VMEM)
    hbm = pl.BlockSpec(memory_space=pl.ANY)
    held = [] if before is None else [before]
    return pl.pallas_call(
        functools.partial(place_kernel, len(pieces), n_z, chunk),
        out_shape=jax.ShapeDtypeStruct((chunks * tokens, columns), BF16),
        in_specs=[pl.BlockSpec(memory_space=pltpu.SMEM)] + [vmem] * len(pieces) + [hbm] * len(held),
        out_specs=hbm,
        scratch_shapes=[pltpu.VMEM((tokens, columns), BF16), pltpu.SemaphoreType.DMA],
        input_output_aliases={1 + len(pieces): 0} if held else {},
        compiler_params=pltpu.CompilerParams(vmem_limit_bytes=12 * MIB),
        cost_estimate=pl.CostEstimate(flops=0, bytes_accessed=4 * tokens * columns, transcendentals=0),
    )(offsets, *pieces, *held)


def body(queries, span_k, span_v, cache_k, cache_v, block_slot, pattern, wo):
    n_z, n_x, n_h = (lax.axis_size(a) for a in ("fsdp", "seq", "head"))
    z, x, me = (lax.axis_index(a) for a in ("fsdp", "seq", "head"))
    chunks, list_len = pattern.shape
    cb_local, block_len, _ = cache_k.shape
    index_here = z * n_x + x
    capacity = min(max(2, 2 * chunks * list_len // (n_z * n_x)), list_len)
    capacity = -(-capacity // 4) * 4

    slots = block_slot[pattern]
    slots = jnp.stack([slots] + [swap(slots, "fsdp", k) for k in range(1, n_z)])
    slots = jnp.stack([slots] + [swap(slots, "seq", s) for s in range(1, n_x)])
    within = slots - index_here * cb_local
    mine = (within >= 0) & (within < cb_local)
    before = jnp.tri(list_len, list_len, -1, dtype=bool)
    rank = jnp.sum((mine[..., None, :] & before).astype(jnp.int32), axis=-1)
    rank = jnp.where(mine, rank, -1)
    chosen = rank[..., None, :] == jnp.arange(capacity)[:, None]
    compact = jnp.sum(jnp.where(chosen, within[..., None, :], 0), axis=-1)
    table = jnp.concatenate([jnp.sum(mine.astype(jnp.int32), axis=-1, keepdims=True), compact], axis=-1)

    prior = lax.ppermute(
        jnp.concatenate([span_k[-block_len:], span_v[-block_len:]], axis=1),
        ("fsdp", "seq"), [(i, i + 1) for i in range(n_z * n_x - 1)],
    )

    quarter = wo.shape[1] // n_h
    picked = jnp.stack([(me ^ j) * quarter for j in range(n_h)])
    offsets = jnp.stack([jnp.stack([(z ^ k) * wo.shape[1] + (me ^ j) * quarter for k in range(n_z)]) for j in range(n_h)])

    last = [queries]

    def run(call, *args):
        result = call(last[0], *args)
        last[0] = result[0] if isinstance(result, (list, tuple)) else result
        return result

    far_first = []
    distance = n_z
    while distance > 1:
        distance //= 2
        far_first.append(distance)
    blocks_of = [slice(c * block_len, (c + 1) * block_len) for c in range(chunks)]

    def over_z(block):
        held = {0: block}
        for distance in far_first:
            for k in list(held):
                held[k ^ distance] = swap(held[k], "fsdp", distance)
        return held

    by_z, gathered, span_parts = [], [], []
    for c in range(chunks):
        by_z.append(over_z(queries[blocks_of[c]]))
        gathered.append({(s, k): swap(q, "seq", s) for k, q in by_z[c].items() for s in range(1, n_x)})
    for c in range(chunks):
        if c == 0:
            k0, v0 = prior[:, :HD], prior[:, HD:]
        else:
            k0, v0 = span_k[blocks_of[c - 1]], span_v[blocks_of[c - 1]]
        flag = (index_here * chunks + c > 0).astype(jnp.int32).reshape(1)
        span_parts.append(run(attend_span, flag, by_z[c][0], k0, span_k[blocks_of[c]], v0, span_v[blocks_of[c]]))

    near = [k for k in range(n_z) if k % 2] or [0]
    rest = [k for k in range(n_z) if k % 2 == 0 and k not in near]
    parts = [{k: [] for k in range(n_z)} for _ in range(chunks)]

    def listed(c, s, ks):
        if not ks:
            return
        queries_of = [by_z[c][k] if s == 0 else gathered[c][s, k] for k in ks]
        rows = jnp.stack([table[s, k, c] for k in ks])
        found = run(attend_listed, rows, queries_of, cache_k, cache_v)
        for k, part in zip(ks, found):
            parts[c][k].append(part if s == 0 else swap(part, "seq", s))

    def away(c, ks):
        for s in range(1, n_x):
            listed(c, s, ks)

    def here(c, ks):
        listed(c, 0, ks)

    def pass_on(c, distance):
        for k in range(n_z):
            if k & distance and k % distance == 0:
                parts[c][k ^ distance].append(swap(run(merge, parts[c][k]), "fsdp", distance))

    def attend(c):
        return run(merge, parts[c][0] + [span_parts[c]], block_len)

    kept = [j for j in range(n_h) if j % 2 == 0] if n_h > 1 else [0]

    def project_sent(c, rows_of):
        return swap(run(project, picked, rows_of, wo, [j ^ 1 for j in kept]), "head", 1) if n_h > 1 else None

    def project_kept(c, rows_of, got):
        held = run(project, picked, rows_of, wo, kept).astype(F32)
        return held if got is None else held + got.astype(F32)

    def reduce_head(held):
        columns, distance = kept, 2
        while distance < n_h:
            stay = [i for i, j in enumerate(columns) if j % (2 * distance) == 0]
            go = [columns.index(columns[i] ^ distance) for i in stay]
            cut = lambda ids: jnp.concatenate([held[:, i * quarter:(i + 1) * quarter] for i in ids], axis=1)
            got = swap(cut(go).astype(BF16), "head", distance)
            held = cut(stay) + got.astype(F32)
            columns = [columns[i] for i in stay]
            distance *= 2
        return held.astype(BF16)

    def spread(summed):
        pieces = {0: jnp.concatenate(
            [summed[:block_len]]
            + [swap(summed[k * block_len:(k + 1) * block_len], "fsdp", k) for k in range(1, n_z)], axis=0
        )}
        distance = n_h
        while distance > 1:
            distance //= 2
            for j in list(pieces):
                pieces[j ^ distance] = swap(pieces[j], "head", distance)
        return [pieces[j] for j in range(n_h)]

    def finish(c, rows_of, mixed):
        got = project_sent(c, rows_of)
        held = project_kept(c, rows_of, got)
        return place(offsets, spread(reduce_head(held)), c, chunks, mixed)

    mixed = None
    waiting = None
    for c in range(chunks):
        if c == 0:
            away(c, rest)
            away(c, near)
            here(c, near)
        if c + 1 < chunks:
            away(c + 1, rest)
        if n_z > 1:
            pass_on(c, 1)
        here(c, rest)
        if c + 1 < chunks:
            away(c + 1, near)
        distance = 2
        while distance < n_z:
            pass_on(c, distance)
            distance *= 2
        if c + 1 < chunks:
            here(c + 1, near)
        attended = attend(c)
        rows_of = over_z(attended)
        rows_of = [rows_of[k] for k in range(n_z)]
        if waiting is not None:
            mixed = finish(waiting[0], waiting[1], mixed)
        waiting = (c, rows_of)
    return finish(waiting[0], waiting[1], mixed)


def solution(mesh):
    return jax.shard_map(
        body,
        mesh=mesh,
        in_specs=(
            P(("fsdp", "seq"), "head"),
            P(("fsdp", "seq"), "head"),
            P(("fsdp", "seq"), "head"),
            P(("fsdp", "seq"), None, "head"),
            P(("fsdp", "seq"), None, "head"),
            P(),
            P(("fsdp", "seq"), None),
            P("head", "fsdp"),
        ),
        out_specs=P(("fsdp", "seq"), None),
        check_vma=False,
    )
```

```python
import functools
import math

import jax
import jax.numpy as jnp
from jax import lax
from jax.experimental import pallas as pl
from jax.experimental.pallas import tpu as pltpu
from jax.sharding import PartitionSpec as P

HD = 128
NEG = -1e30
STATS = 16
F32 = jnp.float32
BF16 = jnp.bfloat16
MIB = 1024 * 1024
LIGHT = pl.CostEstimate(flops=1_000_000_000, bytes_accessed=1_000_000, transcendentals=0)


def swap(value, axis, distance):
    count = lax.axis_size(axis)
    return lax.ppermute(value, axis, [(i, i ^ distance) for i in range(count)])


def stack_heads(q_ref, stacked):
    tokens = q_ref.shape[0]
    for h in range(q_ref.shape[1] // HD):
        rows = slice(h * tokens, (h + 1) * tokens)
        scaled = q_ref[:, h * HD:(h + 1) * HD].astype(F32) * (math.log2(math.e) / math.sqrt(HD))
        high = scaled.astype(BF16)
        stacked[rows, :HD] = high
        stacked[rows, HD:] = (scaled - high.astype(F32)).astype(BF16)


def scores_of(keys, stacked):
    twice = jnp.concatenate([keys, keys], axis=1)
    return lax.dot_general(twice, stacked[...], (((1,), (1,)), ((), ())), preferred_element_type=F32)


def weigh(values, probs):
    return lax.dot_general(values, probs.astype(BF16), (((0,), (0,)), ((), ())), preferred_element_type=F32)


def in_eights(array):
    return array.reshape(array.shape[0] // 8, 8, array.shape[1])


def write_partial(out_ref, acc, total, top):
    inverse = jnp.where(total > 0, 1.0 / total, 0.0)
    out_ref[:HD] = (acc[...] * inverse).astype(BF16)
    write_stats(out_ref, total, top)


def write_stats(out_ref, total, top):
    high = total.astype(BF16).astype(F32)
    row = lax.broadcasted_iota(jnp.int32, (STATS, out_ref.shape[1]), 0)
    stats = jnp.where(row == 0, top, jnp.where(row == 1, high, jnp.where(row == 2, total - high, 0.0)))
    out_ref[HD:] = stats.astype(BF16)


def listed_kernel(blocks, table, *refs):
    q_refs, refs = refs[:blocks], refs[blocks:]
    k_ref, v_ref, refs = refs[0], refs[1], refs[3:]
    out_refs, (stacked, scores, acc) = refs[:blocks], refs[blocks:]
    block_len = k_ref.shape[1]
    columns = stacked.shape[0]
    for j in range(blocks):
        count = table[j, 0]
        stack_heads(q_refs[j], stacked)
        acc[...] = jnp.zeros(acc.shape, F32)

        def first(group, base, i, running):
            at = base + group * i
            keys = jnp.concatenate([k_ref[table[j, 1 + at + g]] for g in range(group)], axis=0)
            found = scores_of(keys, stacked)
            for g in range(group):
                part = found[g * block_len:(g + 1) * block_len]
                if g:
                    part = part + jnp.where(at + g < count, 0.0, NEG).astype(F32)
                scores[at + g] = part
                running = jnp.maximum(running, jnp.max(in_eights(part), axis=0))
            return running

        def second(group, base, i, total):
            at = base + group * i
            found = scores[pl.ds(at, group)].reshape(group * block_len // 8, 8, columns)
            probs = jnp.exp2(found - top_eight[None])
            values = jnp.concatenate([v_ref[table[j, 1 + at + g]] for g in range(group)], axis=0)
            acc[...] += weigh(values, probs.reshape(group * block_len, columns))
            return total + jnp.sum(probs, axis=0)

        def over(step, carry):
            fours = (count + 1) // 4
            carry = lax.fori_loop(0, fours, functools.partial(step, 4, 0), carry)
            rest = (jnp.maximum(count - 4 * fours, 0) + 1) // 2
            return lax.fori_loop(0, rest, functools.partial(step, 2, 4 * fours), carry)

        running = over(first, jnp.full((8, columns), NEG, F32))
        top = jnp.max(running, axis=0, keepdims=True).astype(BF16).astype(F32)
        top_eight = jnp.broadcast_to(top, (8, columns))
        total = jnp.sum(over(second, jnp.zeros((8, columns), F32)), axis=0, keepdims=True)
        write_partial(out_refs[j], acc, total, top)


def attend_listed(after, table, queries, cache_k, cache_v):
    blocks = len(queries)
    tokens, width = queries[0].shape
    columns = tokens * width // HD
    block_len = cache_k.shape[1]
    vmem = pl.BlockSpec(memory_space=pltpu.VMEM)
    keys = blocks * block_len * 6
    return pl.pallas_call(
        functools.partial(listed_kernel, blocks),
        out_shape=[jax.ShapeDtypeStruct((HD + STATS, columns), BF16)] * blocks,
        in_specs=[pl.BlockSpec(memory_space=pltpu.SMEM)] + [vmem] * (blocks + 2) + [pl.BlockSpec(memory_space=pl.ANY)],
        out_specs=[vmem] * blocks,
        scratch_shapes=[
            pltpu.VMEM((columns, 2 * HD), BF16),
            pltpu.VMEM((table.shape[1] - 1, block_len, columns), F32),
            pltpu.VMEM((HD, columns), F32),
        ],
        compiler_params=pltpu.CompilerParams(vmem_limit_bytes=24 * MIB),
        cost_estimate=LIGHT,
    )(table, *queries, cache_k, cache_v, after)


def span_kernel(flag, q_ref, k0, k1, v0, v1, after, out_ref, stacked, acc):
    tokens = q_ref.shape[0]
    stack_heads(q_ref, stacked)
    found = scores_of(jnp.concatenate([k0[...], k1[...]], axis=0), stacked)
    key = lax.broadcasted_iota(jnp.int32, found.shape, 0)
    token = lax.broadcasted_iota(jnp.int32, found.shape, 1) % tokens
    behind = jnp.where(flag[0] > 0, tokens, 0)
    found = jnp.where((key < behind) | ((key >= tokens) & (key - tokens <= token)), found, NEG)
    top = jnp.max(found, axis=0, keepdims=True).astype(BF16).astype(F32)
    probs = jnp.exp2(found - top)
    acc[...] = weigh(jnp.concatenate([v0[...], v1[...]], axis=0), probs)
    write_partial(out_ref, acc, jnp.sum(probs, axis=0, keepdims=True), top)


def attend_span(after, flag, queries, k0, k1, v0, v1):
    tokens, width = queries.shape
    columns = tokens * width // HD
    vmem = pl.BlockSpec(memory_space=pltpu.VMEM)
    return pl.pallas_call(
        span_kernel,
        out_shape=jax.ShapeDtypeStruct((HD + STATS, columns), BF16),
        in_specs=[pl.BlockSpec(memory_space=pltpu.SMEM)] + [vmem] * 5 + [pl.BlockSpec(memory_space=pl.ANY)],
        out_specs=vmem,
        scratch_shapes=[pltpu.VMEM((columns, 2 * HD), BF16), pltpu.VMEM((HD, columns), F32)],
        compiler_params=pltpu.CompilerParams(vmem_limit_bytes=8 * MIB),
        cost_estimate=LIGHT,
    )(flag, queries, k0, k1, v0, v1, after)


def merge_kernel(count, final, *refs):
    parts, out_ref = refs[:count], refs[count + 1]
    stats = [part[HD:].astype(F32) for part in parts]
    tops = [s[0:1] for s in stats]
    top = functools.reduce(jnp.maximum, tops)
    weights = [jnp.exp2(t - top) * (s[1:2] + s[2:3]) for t, s in zip(tops, stats)]
    total = functools.reduce(jnp.add, weights)
    inverse = jnp.where(total > 0, 1.0 / total, 0.0)
    weights = [w * inverse for w in weights]
    tokens = out_ref.shape[0] if final else HD
    for lower in range(0, parts[0].shape[1], tokens):
        columns = slice(lower, lower + tokens)
        joined = functools.reduce(jnp.add, [w[:, columns] * part[:HD, columns].astype(F32) for w, part in zip(weights, parts)])
        if final:
            h = lower // tokens
            out_ref[:, h * HD:(h + 1) * HD] = joined.T.astype(BF16)
        else:
            out_ref[:HD, columns] = joined.astype(BF16)
    if not final:
        write_stats(out_ref, total, top)


def merge(after, parts, tokens=None):
    rows, columns = parts[0].shape
    vmem = pl.BlockSpec(memory_space=pltpu.VMEM)
    shape = (tokens, columns * HD // tokens) if tokens else (rows, columns)
    return pl.pallas_call(
        functools.partial(merge_kernel, len(parts), tokens is not None),
        out_shape=jax.ShapeDtypeStruct(shape, BF16),
        in_specs=[vmem] * len(parts) + [pl.BlockSpec(memory_space=pl.ANY)],
        out_specs=vmem,
        compiler_params=pltpu.CompilerParams(vmem_limit_bytes=8 * MIB),
        cost_estimate=LIGHT,
    )(*parts, after)


def project_kernel(count, picks, has_term, offsets, *refs):
    parts, wo_ref, refs = refs[:count], refs[count], refs[count + 1:]
    term = refs[0] if has_term else None
    out_refs, stacked = refs[has_term + 1:-1], refs[-1]
    tokens = parts[0].shape[0]
    width = out_refs[0].shape[1]
    for k, part in enumerate(parts):
        stacked[k * tokens:(k + 1) * tokens] = part[...]
    for at, j in enumerate(picks):
        start = pl.multiple_of(offsets[j], width)
        found = jnp.dot(stacked[...], wo_ref[:, pl.ds(start, width)], preferred_element_type=F32)
        if has_term:
            found = found + term[:, at * width:(at + 1) * width].astype(F32)
        out_refs[at][...] = found.astype(BF16)


def project(after, offsets, parts, wo, picks, term=None):
    tokens, depth = parts[0].shape
    width = wo.shape[1] // offsets.shape[0]
    rows = len(parts) * tokens
    vmem = pl.BlockSpec(memory_space=pltpu.VMEM)
    terms = [] if term is None else [term]
    return pl.pallas_call(
        functools.partial(project_kernel, len(parts), tuple(picks), len(terms)),
        out_shape=[jax.ShapeDtypeStruct((rows, width), BF16)] * len(picks),
        in_specs=[pl.BlockSpec(memory_space=pltpu.SMEM)] + [vmem] * (len(parts) + 1 + len(terms)) + [pl.BlockSpec(memory_space=pl.ANY)],
        out_specs=[vmem] * len(picks),
        scratch_shapes=[pltpu.VMEM((rows, depth), BF16)],
        compiler_params=pltpu.CompilerParams(vmem_limit_bytes=10 * MIB),
        cost_estimate=LIGHT,
    )(offsets, *parts, wo, *terms, after)


def send_kernel(count, picks, offsets, *refs):
    parts, wo_ref, out_ref, stacked = refs[:count], refs[count], refs[count + 2], refs[count + 3]
    tokens = parts[0].shape[0]
    width = out_ref.shape[1] // len(picks)
    for k, part in enumerate(parts):
        stacked[k * tokens:(k + 1) * tokens] = part[...]
    for at, j in enumerate(picks):
        start = pl.multiple_of(offsets[j], width)
        out_ref[:, at * width:(at + 1) * width] = jnp.dot(
            stacked[...], wo_ref[:, pl.ds(start, width)], preferred_element_type=F32
        ).astype(BF16)


def project_side(after, offsets, parts, wo, picks):
    tokens, depth = parts[0].shape
    rows = len(parts) * tokens
    vmem = pl.BlockSpec(memory_space=pltpu.VMEM)
    return pl.pallas_call(
        functools.partial(send_kernel, len(parts), tuple(picks)),
        out_shape=jax.ShapeDtypeStruct((rows, wo.shape[1] // offsets.shape[0] * len(picks)), BF16),
        in_specs=[pl.BlockSpec(memory_space=pltpu.SMEM)] + [vmem] * (len(parts) + 1) + [pl.BlockSpec(memory_space=pl.ANY)],
        out_specs=vmem,
        scratch_shapes=[pltpu.VMEM((rows, depth), BF16)],
        compiler_params=pltpu.CompilerParams(vmem_limit_bytes=10 * MIB),
        cost_estimate=LIGHT,
    )(offsets, *parts, wo, after)


def add_kernel(splits, one, two, after, *out_refs):
    total = (one[...].astype(F32) + two[...].astype(F32)).astype(BF16)
    rows = total.shape[0] // splits
    for i, out_ref in enumerate(out_refs):
        out_ref[...] = total[i * rows:(i + 1) * rows]


def add(after, one, two, splits):
    rows, width = one.shape
    vmem = pl.BlockSpec(memory_space=pltpu.VMEM)
    return pl.pallas_call(
        functools.partial(add_kernel, splits),
        out_shape=[jax.ShapeDtypeStruct((rows // splits, width), BF16)] * splits,
        in_specs=[vmem] * 2 + [pl.BlockSpec(memory_space=pl.ANY)],
        out_specs=[vmem] * splits,
        compiler_params=pltpu.CompilerParams(vmem_limit_bytes=8 * MIB),
        cost_estimate=LIGHT,
    )(one, two, after)


def join_kernel(after, *refs):
    sources, out_ref = refs[:-1], refs[-1]
    rows = sources[0].shape[0]
    for i, source in enumerate(sources):
        out_ref[i * rows:(i + 1) * rows] = source[...]


def join(after, sources):
    rows, width = sources[0].shape
    vmem = pl.BlockSpec(memory_space=pltpu.VMEM)
    return pl.pallas_call(
        join_kernel,
        out_shape=jax.ShapeDtypeStruct((len(sources) * rows, width), BF16),
        in_specs=[pl.BlockSpec(memory_space=pl.ANY)] + [vmem] * len(sources),
        out_specs=vmem,
        compiler_params=pltpu.CompilerParams(vmem_limit_bytes=8 * MIB),
        cost_estimate=LIGHT,
    )(after, *sources)


def place_kernel(blocks, chunk, tokens, offsets, *refs):
    out_ref, sem = refs[-2:]
    copies = []
    for ref, at, j, k in blocks:
        width = refs[ref].shape[1]
        start = pl.multiple_of(offsets[j, k], width)
        copies.append(pltpu.make_async_copy(
            refs[ref].at[pl.ds(at * tokens, tokens)],
            out_ref.at[pl.ds(chunk * tokens, tokens), pl.ds(start, width)],
            sem.at[len(copies)],
        ))
    for copy in copies:
        copy.start()
    for copy in copies:
        copy.wait()


def place(after, offsets, arrays, blocks, chunk, tokens, shape, before):
    vmem = pl.BlockSpec(memory_space=pltpu.VMEM)
    hbm = pl.BlockSpec(memory_space=pl.ANY)
    held = [] if before is None else [before]
    return pl.pallas_call(
        functools.partial(place_kernel, tuple(blocks), chunk, tokens),
        out_shape=jax.ShapeDtypeStruct(shape, BF16),
        in_specs=[pl.BlockSpec(memory_space=pltpu.SMEM)] + [vmem] * len(arrays) + [hbm] * (1 + len(held)),
        out_specs=hbm,
        scratch_shapes=[pltpu.SemaphoreType.DMA((len(blocks),))],
        input_output_aliases={1 + len(arrays): 0} if held else {},
        compiler_params=pltpu.CompilerParams(vmem_limit_bytes=8 * MIB),
        cost_estimate=LIGHT,
    )(offsets, *arrays, *held, after)


def body(queries, span_k, span_v, cache_k, cache_v, block_slot, pattern, wo):
    n_z, n_x, n_h = (lax.axis_size(a) for a in ("fsdp", "seq", "head"))
    z, x, me = (lax.axis_index(a) for a in ("fsdp", "seq", "head"))
    chunks, list_len = pattern.shape
    cb_local, block_len, _ = cache_k.shape
    index_here = z * n_x + x
    capacity = min(max(2, 2 * chunks * list_len // (n_z * n_x)), list_len)
    capacity = -(-capacity // 4) * 4

    slots = block_slot[pattern]
    slots = jnp.stack([slots] + [swap(slots, "fsdp", k) for k in range(1, n_z)])
    slots = jnp.stack([slots] + [swap(slots, "seq", s) for s in range(1, n_x)])
    within = slots - index_here * cb_local
    mine = (within >= 0) & (within < cb_local)
    before = jnp.tri(list_len, list_len, -1, dtype=bool)
    rank = jnp.sum((mine[..., None, :] & before).astype(jnp.int32), axis=-1)
    rank = jnp.where(mine, rank, -1)
    chosen = rank[..., None, :] == jnp.arange(capacity)[:, None]
    compact = jnp.sum(jnp.where(chosen, within[..., None, :], 0), axis=-1)
    table = jnp.concatenate([jnp.sum(mine.astype(jnp.int32), axis=-1, keepdims=True), compact], axis=-1)

    prior = lax.ppermute(
        jnp.concatenate([span_k[-block_len:], span_v[-block_len:]], axis=1),
        ("fsdp", "seq"), [(i, i + 1) for i in range(n_z * n_x - 1)],
    )

    quarter = wo.shape[1] // n_h
    picked = jnp.stack([(me ^ j) * quarter for j in range(n_h)])
    offsets = jnp.stack([jnp.stack([(z ^ k) * wo.shape[1] + (me ^ j) * quarter for k in range(n_z)]) for j in range(n_h)])

    last = [queries]

    def run(call, *args):
        result = call(last[0], *args)
        if call is not place:
            last[0] = result[0] if isinstance(result, (list, tuple)) else result
        return result

    far_first = []
    distance = n_z
    while distance > 1:
        distance //= 2
        far_first.append(distance)
    blocks_of = [slice(c * block_len, (c + 1) * block_len) for c in range(chunks)]

    def over_z(block):
        held = {0: block}
        for distance in far_first:
            for k in list(held):
                held[k ^ distance] = swap(held[k], "fsdp", distance)
        return held

    by_z, gathered, span_parts = [], [], []
    for c in range(chunks):
        by_z.append(over_z(queries[blocks_of[c]]))
        gathered.append({(s, k): swap(q, "seq", s) for k, q in by_z[c].items() for s in range(1, n_x)})
    for c in range(chunks):
        if c == 0:
            k0, v0 = prior[:, :HD], prior[:, HD:]
        else:
            k0, v0 = span_k[blocks_of[c - 1]], span_v[blocks_of[c - 1]]
        flag = (index_here * chunks + c > 0).astype(jnp.int32).reshape(1)
        span_parts.append(run(attend_span, flag, by_z[c][0], k0, span_k[blocks_of[c]], v0, span_v[blocks_of[c]]))

    near = [k for k in range(n_z) if k % 2] or [0]
    rest = [k for k in range(n_z) if k % 2 == 0 and k not in near]
    parts = [{k: [] for k in range(n_z)} for _ in range(chunks)]

    def listed(c, s, ks):
        if not ks:
            return
        queries_of = [by_z[c][k] if s == 0 else gathered[c][s, k] for k in ks]
        rows = jnp.stack([table[s, k, c] for k in ks])
        found = run(attend_listed, rows, queries_of, cache_k, cache_v)
        for k, part in zip(ks, found):
            parts[c][k].append(part if s == 0 else swap(part, "seq", s))

    def away(c, ks):
        for s in range(1, n_x):
            listed(c, s, ks)

    def here(c, ks):
        listed(c, 0, ks)

    def pass_on(c, distance):
        for k in range(n_z):
            if k & distance and k % distance == 0:
                parts[c][k ^ distance].append(swap(run(merge, parts[c][k]), "fsdp", distance))

    def merge_to(c, k, distance):
        parts[c][k ^ distance].append(swap(run(merge, parts[c][k]), "fsdp", distance))

    attended = {}

    def attend(c):
        attended[c] = over_z(run(merge, parts[c][0] + [span_parts[c]], block_len))

    even = [j for j in range(n_h) if j % 2 == 0]
    odd = [j ^ 1 for j in even]
    state = {}
    shape = (chunks * block_len, n_z * wo.shape[1])

    def project_sent(c, ks):
        rows_of = [attended[c][k] for k in ks]
        state[c, ks[0]] = swap(run(project_side, picked, rows_of, wo, odd), "head", 1)

    def project_kept(c, ks):
        rows_of = [attended[c][k] for k in ks]
        held = dict(zip(even, run(project, picked, rows_of, wo, even, state[c, ks[0]])))
        state[c, ks[0]] = (held[0], swap(held[2], "head", 2))

    def total(c, ks):
        rows_of = run(add, *state[c, ks[0]], len(ks))
        state[c, ks[0]] = [swap(r, "fsdp", k) if k else r for k, r in zip(ks, rows_of)]

    def spread(c, ks):
        first = run(join, state[c, ks[0]])
        state[c, ks[0]] = [first, swap(first, "head", 2)]

    def spread_on(c, ks):
        both = run(join, state[c, ks[0]])
        state[c, ks[0]] = [both, swap(both, "head", 1)]

    mixed = [None]

    def put(c, ks):
        blocks = [
            (ref, at * len(ks) + i, j, k)
            for ref, columns in enumerate((even, odd)) for at, j in enumerate(columns) for i, k in enumerate(ks)
        ]
        mixed[0] = run(place, offsets, state[c, ks[0]], blocks, c, block_len, shape, mixed[0])

    low, high, whole = list(range(n_z // 2)), list(range(n_z // 2, n_z)), list(range(n_z))
    assert chunks == 2 and n_z == 4 and n_h == 4
    A, B = 0, 1
    away(A, rest)
    away(A, near)
    here(A, near)
    away(B, rest)
    merge_to(A, 1, 1)
    merge_to(A, 3, 1)
    here(A, rest)
    away(B, near)
    merge_to(A, 2, 2)
    here(B, near)
    attend(A)
    merge_to(B, 1, 1)
    merge_to(B, 3, 1)
    here(B, rest)
    merge_to(B, 2, 2)
    project_sent(A, whole)
    project_kept(A, whole)
    attend(B)
    total(A, whole)
    project_sent(B, whole)
    project_kept(B, whole)
    spread(A, whole)
    total(B, whole)
    spread_on(A, whole)
    spread(B, whole)
    put(A, whole)
    spread_on(B, whole)
    put(B, whole)
    return mixed[0]


def solution(mesh):
    return jax.shard_map(
        body,
        mesh=mesh,
        in_specs=(
            P(("fsdp", "seq"), "head"),
            P(("fsdp", "seq"), "head"),
            P(("fsdp", "seq"), "head"),
            P(("fsdp", "seq"), None, "head"),
            P(("fsdp", "seq"), None, "head"),
            P(),
            P(("fsdp", "seq"), None),
            P("head", "fsdp"),
        ),
        out_specs=P(("fsdp", "seq"), None),
        check_vma=False,
    )
```

```python
import functools
import math

import jax
import jax.numpy as jnp
from jax import lax
from jax.experimental import pallas as pl
from jax.experimental.pallas import tpu as pltpu
from jax.sharding import PartitionSpec as P

HD = 128
NEG = -1e30
STATS = 16
F32 = jnp.float32
BF16 = jnp.bfloat16
MIB = 1024 * 1024
LIGHT = pl.CostEstimate(flops=1_000_000_000, bytes_accessed=1_000_000, transcendentals=0)


def swap(value, axis, distance):
    count = lax.axis_size(axis)
    return lax.ppermute(value, axis, [(i, i ^ distance) for i in range(count)])


def stack_heads(q_ref, stacked):
    tokens = q_ref.shape[0]
    for h in range(q_ref.shape[1] // HD):
        rows = slice(h * tokens, (h + 1) * tokens)
        scaled = q_ref[:, h * HD:(h + 1) * HD].astype(F32) * (math.log2(math.e) / math.sqrt(HD))
        high = scaled.astype(BF16)
        stacked[rows, :HD] = high
        stacked[rows, HD:] = (scaled - high.astype(F32)).astype(BF16)


def scores_of(keys, stacked):
    twice = jnp.concatenate([keys, keys], axis=1)
    return lax.dot_general(twice, stacked[...], (((1,), (1,)), ((), ())), preferred_element_type=F32)


def weigh(values, probs):
    return lax.dot_general(values, probs.astype(BF16), (((0,), (0,)), ((), ())), preferred_element_type=F32)


def in_eights(array):
    return array.reshape(array.shape[0] // 8, 8, array.shape[1])


def write_partial(out_ref, acc, total, top):
    inverse = jnp.where(total > 0, 1.0 / total, 0.0)
    out_ref[:HD] = (acc[...] * inverse).astype(BF16)
    write_stats(out_ref, total, top)


def write_stats(out_ref, total, top):
    high = total.astype(BF16).astype(F32)
    row = lax.broadcasted_iota(jnp.int32, (STATS, out_ref.shape[1]), 0)
    stats = jnp.where(row == 0, top, jnp.where(row == 1, high, jnp.where(row == 2, total - high, 0.0)))
    out_ref[HD:] = stats.astype(BF16)


def listed_kernel(blocks, table, *refs):
    q_refs, refs = refs[:blocks], refs[blocks:]
    k_ref, v_ref, refs = refs[0], refs[1], refs[3:]
    out_refs, (stacked, scores, acc) = refs[:blocks], refs[blocks:]
    block_len = k_ref.shape[1]
    columns = stacked.shape[0]
    for j in range(blocks):
        count = table[j, 0]
        stack_heads(q_refs[j], stacked)
        acc[...] = jnp.zeros(acc.shape, F32)

        def first(group, base, i, running):
            at = base + group * i
            keys = jnp.concatenate([k_ref[table[j, 1 + at + g]] for g in range(group)], axis=0)
            found = scores_of(keys, stacked)
            for g in range(group):
                part = found[g * block_len:(g + 1) * block_len]
                if g:
                    part = part + jnp.where(at + g < count, 0.0, NEG).astype(F32)
                scores[at + g] = part
                running = jnp.maximum(running, jnp.max(in_eights(part), axis=0))
            return running

        def second(group, base, i, total):
            at = base + group * i
            found = scores[pl.ds(at, group)].reshape(group * block_len // 8, 8, columns)
            probs = jnp.exp2(found - top_eight[None])
            values = jnp.concatenate([v_ref[table[j, 1 + at + g]] for g in range(group)], axis=0)
            acc[...] += weigh(values, probs.reshape(group * block_len, columns))
            return total + jnp.sum(probs, axis=0)

        def over(step, carry):
            fours = (count + 1) // 4
            carry = lax.fori_loop(0, fours, functools.partial(step, 4, 0), carry)
            rest = (jnp.maximum(count - 4 * fours, 0) + 1) // 2
            return lax.fori_loop(0, rest, functools.partial(step, 2, 4 * fours), carry)

        running = over(first, jnp.full((8, columns), NEG, F32))
        top = jnp.max(running, axis=0, keepdims=True).astype(BF16).astype(F32)
        top_eight = jnp.broadcast_to(top, (8, columns))
        total = jnp.sum(over(second, jnp.zeros((8, columns), F32)), axis=0, keepdims=True)
        write_partial(out_refs[j], acc, total, top)


def attend_listed(after, table, queries, cache_k, cache_v):
    blocks = len(queries)
    tokens, width = queries[0].shape
    columns = tokens * width // HD
    block_len = cache_k.shape[1]
    vmem = pl.BlockSpec(memory_space=pltpu.VMEM)
    keys = blocks * block_len * 6
    return pl.pallas_call(
        functools.partial(listed_kernel, blocks),
        out_shape=[jax.ShapeDtypeStruct((HD + STATS, columns), BF16)] * blocks,
        in_specs=[pl.BlockSpec(memory_space=pltpu.SMEM)] + [vmem] * (blocks + 2) + [pl.BlockSpec(memory_space=pl.ANY)],
        out_specs=[vmem] * blocks,
        scratch_shapes=[
            pltpu.VMEM((columns, 2 * HD), BF16),
            pltpu.VMEM((table.shape[1] - 1, block_len, columns), F32),
            pltpu.VMEM((HD, columns), F32),
        ],
        compiler_params=pltpu.CompilerParams(vmem_limit_bytes=24 * MIB),
        cost_estimate=LIGHT,
    )(table, *queries, cache_k, cache_v, after)


def span_kernel(flag, q_ref, k0, k1, v0, v1, after, out_ref, stacked, acc):
    tokens = q_ref.shape[0]
    stack_heads(q_ref, stacked)
    found = scores_of(jnp.concatenate([k0[...], k1[...]], axis=0), stacked)
    key = lax.broadcasted_iota(jnp.int32, found.shape, 0)
    token = lax.broadcasted_iota(jnp.int32, found.shape, 1) % tokens
    behind = jnp.where(flag[0] > 0, tokens, 0)
    found = jnp.where((key < behind) | ((key >= tokens) & (key - tokens <= token)), found, NEG)
    top = jnp.max(found, axis=0, keepdims=True).astype(BF16).astype(F32)
    probs = jnp.exp2(found - top)
    acc[...] = weigh(jnp.concatenate([v0[...], v1[...]], axis=0), probs)
    write_partial(out_ref, acc, jnp.sum(probs, axis=0, keepdims=True), top)


def attend_span(after, flag, queries, k0, k1, v0, v1):
    tokens, width = queries.shape
    columns = tokens * width // HD
    vmem = pl.BlockSpec(memory_space=pltpu.VMEM)
    return pl.pallas_call(
        span_kernel,
        out_shape=jax.ShapeDtypeStruct((HD + STATS, columns), BF16),
        in_specs=[pl.BlockSpec(memory_space=pltpu.SMEM)] + [vmem] * 5 + [pl.BlockSpec(memory_space=pl.ANY)],
        out_specs=vmem,
        scratch_shapes=[pltpu.VMEM((columns, 2 * HD), BF16), pltpu.VMEM((HD, columns), F32)],
        compiler_params=pltpu.CompilerParams(vmem_limit_bytes=8 * MIB),
        cost_estimate=LIGHT,
    )(flag, queries, k0, k1, v0, v1, after)


def merge_kernel(count, final, *refs):
    parts, out_ref = refs[:count], refs[count + 1]
    stats = [part[HD:].astype(F32) for part in parts]
    tops = [s[0:1] for s in stats]
    top = functools.reduce(jnp.maximum, tops)
    weights = [jnp.exp2(t - top) * (s[1:2] + s[2:3]) for t, s in zip(tops, stats)]
    total = functools.reduce(jnp.add, weights)
    inverse = jnp.where(total > 0, 1.0 / total, 0.0)
    weights = [w * inverse for w in weights]
    tokens = out_ref.shape[0] if final else HD
    for lower in range(0, parts[0].shape[1], tokens):
        columns = slice(lower, lower + tokens)
        joined = functools.reduce(jnp.add, [w[:, columns] * part[:HD, columns].astype(F32) for w, part in zip(weights, parts)])
        if final:
            h = lower // tokens
            out_ref[:, h * HD:(h + 1) * HD] = joined.T.astype(BF16)
        else:
            out_ref[:HD, columns] = joined.astype(BF16)
    if not final:
        write_stats(out_ref, total, top)


def merge(after, parts, tokens=None):
    rows, columns = parts[0].shape
    vmem = pl.BlockSpec(memory_space=pltpu.VMEM)
    shape = (tokens, columns * HD // tokens) if tokens else (rows, columns)
    return pl.pallas_call(
        functools.partial(merge_kernel, len(parts), tokens is not None),
        out_shape=jax.ShapeDtypeStruct(shape, BF16),
        in_specs=[vmem] * len(parts) + [pl.BlockSpec(memory_space=pl.ANY)],
        out_specs=vmem,
        compiler_params=pltpu.CompilerParams(vmem_limit_bytes=8 * MIB),
        cost_estimate=LIGHT,
    )(*parts, after)


def project_kernel(count, picks, has_term, offsets, *refs):
    parts, wo_ref, refs = refs[:count], refs[count], refs[count + 1:]
    term = refs[0] if has_term else None
    out_refs, stacked = refs[has_term + 1:-1], refs[-1]
    tokens = parts[0].shape[0]
    width = out_refs[0].shape[1]
    for k, part in enumerate(parts):
        stacked[k * tokens:(k + 1) * tokens] = part[...]
    for at, j in enumerate(picks):
        start = pl.multiple_of(offsets[j], width)
        found = jnp.dot(stacked[...], wo_ref[:, pl.ds(start, width)], preferred_element_type=F32)
        if has_term:
            found = found + term[:, at * width:(at + 1) * width].astype(F32)
        out_refs[at][...] = found.astype(BF16)


def project(after, offsets, parts, wo, picks, term=None):
    tokens, depth = parts[0].shape
    width = wo.shape[1] // offsets.shape[0]
    rows = len(parts) * tokens
    vmem = pl.BlockSpec(memory_space=pltpu.VMEM)
    terms = [] if term is None else [term]
    return pl.pallas_call(
        functools.partial(project_kernel, len(parts), tuple(picks), len(terms)),
        out_shape=[jax.ShapeDtypeStruct((rows, width), BF16)] * len(picks),
        in_specs=[pl.BlockSpec(memory_space=pltpu.SMEM)] + [vmem] * (len(parts) + 1 + len(terms)) + [pl.BlockSpec(memory_space=pl.ANY)],
        out_specs=[vmem] * len(picks),
        scratch_shapes=[pltpu.VMEM((rows, depth), BF16)],
        compiler_params=pltpu.CompilerParams(vmem_limit_bytes=10 * MIB),
        cost_estimate=LIGHT,
    )(offsets, *parts, wo, *terms, after)


def send_kernel(count, picks, offsets, *refs):
    parts, wo_ref, out_ref, stacked = refs[:count], refs[count], refs[count + 2], refs[count + 3]
    tokens = parts[0].shape[0]
    width = out_ref.shape[1] // len(picks)
    for k, part in enumerate(parts):
        stacked[k * tokens:(k + 1) * tokens] = part[...]
    for at, j in enumerate(picks):
        start = pl.multiple_of(offsets[j], width)
        out_ref[:, at * width:(at + 1) * width] = jnp.dot(
            stacked[...], wo_ref[:, pl.ds(start, width)], preferred_element_type=F32
        ).astype(BF16)


def project_side(after, offsets, parts, wo, picks):
    tokens, depth = parts[0].shape
    rows = len(parts) * tokens
    vmem = pl.BlockSpec(memory_space=pltpu.VMEM)
    return pl.pallas_call(
        functools.partial(send_kernel, len(parts), tuple(picks)),
        out_shape=jax.ShapeDtypeStruct((rows, wo.shape[1] // offsets.shape[0] * len(picks)), BF16),
        in_specs=[pl.BlockSpec(memory_space=pltpu.SMEM)] + [vmem] * (len(parts) + 1) + [pl.BlockSpec(memory_space=pl.ANY)],
        out_specs=vmem,
        scratch_shapes=[pltpu.VMEM((rows, depth), BF16)],
        compiler_params=pltpu.CompilerParams(vmem_limit_bytes=10 * MIB),
        cost_estimate=LIGHT,
    )(offsets, *parts, wo, after)


def add_kernel(splits, one, two, after, *out_refs):
    total = (one[...].astype(F32) + two[...].astype(F32)).astype(BF16)
    rows = total.shape[0] // splits
    for i, out_ref in enumerate(out_refs):
        out_ref[...] = total[i * rows:(i + 1) * rows]


def add(after, one, two, splits):
    rows, width = one.shape
    vmem = pl.BlockSpec(memory_space=pltpu.VMEM)
    return pl.pallas_call(
        functools.partial(add_kernel, splits),
        out_shape=[jax.ShapeDtypeStruct((rows // splits, width), BF16)] * splits,
        in_specs=[vmem] * 2 + [pl.BlockSpec(memory_space=pl.ANY)],
        out_specs=[vmem] * splits,
        compiler_params=pltpu.CompilerParams(vmem_limit_bytes=8 * MIB),
        cost_estimate=LIGHT,
    )(one, two, after)


def join_kernel(after, *refs):
    sources, out_ref = refs[:-1], refs[-1]
    rows = sources[0].shape[0]
    for i, source in enumerate(sources):
        out_ref[i * rows:(i + 1) * rows] = source[...]


def join(after, sources):
    rows, width = sources[0].shape
    vmem = pl.BlockSpec(memory_space=pltpu.VMEM)
    return pl.pallas_call(
        join_kernel,
        out_shape=jax.ShapeDtypeStruct((len(sources) * rows, width), BF16),
        in_specs=[pl.BlockSpec(memory_space=pl.ANY)] + [vmem] * len(sources),
        out_specs=vmem,
        compiler_params=pltpu.CompilerParams(vmem_limit_bytes=8 * MIB),
        cost_estimate=LIGHT,
    )(after, *sources)


def place_kernel(blocks, chunk, tokens, offsets, *refs):
    out_ref, sem = refs[-2:]
    copies = []
    for ref, at, j, k in blocks:
        width = refs[ref].shape[1]
        start = pl.multiple_of(offsets[j, k], width)
        copies.append(pltpu.make_async_copy(
            refs[ref].at[pl.ds(at * tokens, tokens)],
            out_ref.at[pl.ds(chunk * tokens, tokens), pl.ds(start, width)],
            sem.at[len(copies)],
        ))
    for copy in copies:
        copy.start()
    for copy in copies:
        copy.wait()


def place(after, offsets, arrays, blocks, chunk, tokens, shape, before):
    vmem = pl.BlockSpec(memory_space=pltpu.VMEM)
    hbm = pl.BlockSpec(memory_space=pl.ANY)
    held = [] if before is None else [before]
    return pl.pallas_call(
        functools.partial(place_kernel, tuple(blocks), chunk, tokens),
        out_shape=jax.ShapeDtypeStruct(shape, BF16),
        in_specs=[pl.BlockSpec(memory_space=pltpu.SMEM)] + [vmem] * len(arrays) + [hbm] * (1 + len(held)),
        out_specs=hbm,
        scratch_shapes=[pltpu.SemaphoreType.DMA((len(blocks),))],
        input_output_aliases={1 + len(arrays): 0} if held else {},
        compiler_params=pltpu.CompilerParams(vmem_limit_bytes=8 * MIB),
        cost_estimate=LIGHT,
    )(offsets, *arrays, *held, after)


def body(queries, span_k, span_v, cache_k, cache_v, block_slot, pattern, wo):
    n_z, n_x, n_h = (lax.axis_size(a) for a in ("fsdp", "seq", "head"))
    z, x, me = (lax.axis_index(a) for a in ("fsdp", "seq", "head"))
    chunks, list_len = pattern.shape
    cb_local, block_len, _ = cache_k.shape
    index_here = z * n_x + x
    capacity = min(max(2, 2 * chunks * list_len // (n_z * n_x)), list_len)
    capacity = -(-capacity // 4) * 4

    slots = block_slot[pattern]
    slots = jnp.stack([slots] + [swap(slots, "fsdp", k) for k in range(1, n_z)])
    slots = jnp.stack([slots] + [swap(slots, "seq", s) for s in range(1, n_x)])
    within = slots - index_here * cb_local
    mine = (within >= 0) & (within < cb_local)
    before = jnp.tri(list_len, list_len, -1, dtype=bool)
    rank = jnp.sum((mine[..., None, :] & before).astype(jnp.int32), axis=-1)
    rank = jnp.where(mine, rank, -1)
    chosen = rank[..., None, :] == jnp.arange(capacity)[:, None]
    compact = jnp.sum(jnp.where(chosen, within[..., None, :], 0), axis=-1)
    table = jnp.concatenate([jnp.sum(mine.astype(jnp.int32), axis=-1, keepdims=True), compact], axis=-1)

    prior = lax.ppermute(
        jnp.concatenate([span_k[-block_len:], span_v[-block_len:]], axis=1),
        ("fsdp", "seq"), [(i, i + 1) for i in range(n_z * n_x - 1)],
    )

    quarter = wo.shape[1] // n_h
    picked = jnp.stack([(me ^ j) * quarter for j in range(n_h)])
    offsets = jnp.stack([jnp.stack([(z ^ k) * wo.shape[1] + (me ^ j) * quarter for k in range(n_z)]) for j in range(n_h)])

    last = [queries]

    def run(call, *args):
        result = call(last[0], *args)
        if call is not place:
            last[0] = result[0] if isinstance(result, (list, tuple)) else result
        return result

    far_first = []
    distance = n_z
    while distance > 1:
        distance //= 2
        far_first.append(distance)
    blocks_of = [slice(c * block_len, (c + 1) * block_len) for c in range(chunks)]

    def over_z(block):
        held = {0: block}
        for distance in far_first:
            for k in list(held):
                held[k ^ distance] = swap(held[k], "fsdp", distance)
        return held

    by_z, gathered, span_parts = [], [], []
    for c in range(chunks):
        by_z.append(over_z(queries[blocks_of[c]]))
        gathered.append({(s, k): swap(q, "seq", s) for k, q in by_z[c].items() for s in range(1, n_x)})
    for c in range(chunks):
        if c == 0:
            k0, v0 = prior[:, :HD], prior[:, HD:]
        else:
            k0, v0 = span_k[blocks_of[c - 1]], span_v[blocks_of[c - 1]]
        flag = (index_here * chunks + c > 0).astype(jnp.int32).reshape(1)
        span_parts.append(run(attend_span, flag, by_z[c][0], k0, span_k[blocks_of[c]], v0, span_v[blocks_of[c]]))

    near = [k for k in range(n_z) if k % 2] or [0]
    rest = [k for k in range(n_z) if k % 2 == 0 and k not in near]
    parts = [{k: [] for k in range(n_z)} for _ in range(chunks)]

    def listed(c, s, ks):
        if not ks:
            return
        queries_of = [by_z[c][k] if s == 0 else gathered[c][s, k] for k in ks]
        rows = jnp.stack([table[s, k, c] for k in ks])
        found = run(attend_listed, rows, queries_of, cache_k, cache_v)
        for k, part in zip(ks, found):
            parts[c][k].append(part if s == 0 else swap(part, "seq", s))

    def away(c, ks):
        for s in range(1, n_x):
            listed(c, s, ks)

    def here(c, ks):
        listed(c, 0, ks)

    def pass_on(c, distance):
        for k in range(n_z):
            if k & distance and k % distance == 0:
                parts[c][k ^ distance].append(swap(run(merge, parts[c][k]), "fsdp", distance))

    def merge_to(c, k, distance):
        parts[c][k ^ distance].append(swap(run(merge, parts[c][k]), "fsdp", distance))

    attended = {}

    def attend(c):
        attended[c] = over_z(run(merge, parts[c][0] + [span_parts[c]], block_len))

    even = [j for j in range(n_h) if j % 2 == 0]
    odd = [j ^ 1 for j in even]
    state = {}
    shape = (chunks * block_len, n_z * wo.shape[1])

    def project_sent(c, ks):
        rows_of = [attended[c][k] for k in ks]
        state[c, ks[0]] = swap(run(project_side, picked, rows_of, wo, odd), "head", 1)

    def project_kept(c, ks):
        rows_of = [attended[c][k] for k in ks]
        held = dict(zip(even, run(project, picked, rows_of, wo, even, state[c, ks[0]])))
        state[c, ks[0]] = (held[0], swap(held[2], "head", 2))

    def total(c, ks):
        rows_of = run(add, *state[c, ks[0]], len(ks))
        state[c, ks[0]] = [swap(r, "fsdp", k) if k else r for k, r in zip(ks, rows_of)]

    def spread(c, ks):
        first = run(join, state[c, ks[0]])
        state[c, ks[0]] = [first, swap(first, "head", 2)]

    def spread_on(c, ks):
        both = run(join, state[c, ks[0]])
        state[c, ks[0]] = [both, swap(both, "head", 1)]

    mixed = [None]

    def put(c, ks):
        blocks = [
            (ref, at * len(ks) + i, j, k)
            for ref, columns in enumerate((even, odd)) for at, j in enumerate(columns) for i, k in enumerate(ks)
        ]
        mixed[0] = run(place, offsets, state[c, ks[0]], blocks, c, block_len, shape, mixed[0])

    low, high, whole = list(range(n_z // 2)), list(range(n_z // 2, n_z)), list(range(n_z))
    assert chunks == 2 and n_z == 4 and n_h == 4
    A, B = 0, 1
    away(A, rest)
    away(A, near)
    here(A, near)
    away(B, rest)
    merge_to(A, 1, 1)
    merge_to(A, 3, 1)
    here(A, rest)
    merge_to(A, 2, 2)
    away(B, near)
    here(B, near)
    attend(A)
    merge_to(B, 1, 1)
    merge_to(B, 3, 1)
    here(B, rest)
    merge_to(B, 2, 2)
    project_sent(A, whole)
    project_kept(A, whole)
    attend(B)
    total(A, whole)
    project_sent(B, whole)
    project_kept(B, whole)
    spread(A, whole)
    total(B, whole)
    spread_on(A, whole)
    spread(B, whole)
    put(A, whole)
    spread_on(B, whole)
    put(B, whole)
    return mixed[0]


def solution(mesh):
    return jax.shard_map(
        body,
        mesh=mesh,
        in_specs=(
            P(("fsdp", "seq"), "head"),
            P(("fsdp", "seq"), "head"),
            P(("fsdp", "seq"), "head"),
            P(("fsdp", "seq"), None, "head"),
            P(("fsdp", "seq"), None, "head"),
            P(),
            P(("fsdp", "seq"), None),
            P("head", "fsdp"),
        ),
        out_specs=P(("fsdp", "seq"), None),
        check_vma=False,
    )
```

```python
import functools
import math

import jax
import jax.numpy as jnp
from jax import lax
from jax.experimental import pallas as pl
from jax.experimental.pallas import tpu as pltpu
from jax.sharding import PartitionSpec as P

HD = 128
NEG = -1e30
STATS = 16
F32 = jnp.float32
BF16 = jnp.bfloat16
MIB = 1024 * 1024
LIGHT = pl.CostEstimate(flops=1_000_000_000, bytes_accessed=1_000_000, transcendentals=0)


def swap(value, axis, distance):
    count = lax.axis_size(axis)
    return lax.ppermute(value, axis, [(i, i ^ distance) for i in range(count)])


def stack_heads(q_ref, stacked):
    tokens = q_ref.shape[0]
    for h in range(q_ref.shape[1] // HD):
        rows = slice(h * tokens, (h + 1) * tokens)
        scaled = q_ref[:, h * HD:(h + 1) * HD].astype(F32) * (math.log2(math.e) / math.sqrt(HD))
        high = scaled.astype(BF16)
        stacked[rows, :HD] = high
        stacked[rows, HD:] = (scaled - high.astype(F32)).astype(BF16)


def scores_of(keys, stacked):
    twice = jnp.concatenate([keys, keys], axis=1)
    return lax.dot_general(twice, stacked[...], (((1,), (1,)), ((), ())), preferred_element_type=F32)


def weigh(values, probs):
    return lax.dot_general(values, probs.astype(BF16), (((0,), (0,)), ((), ())), preferred_element_type=F32)


def in_eights(array):
    return array.reshape(array.shape[0] // 8, 8, array.shape[1])


def write_partial(out_ref, acc, total, top):
    inverse = jnp.where(total > 0, 1.0 / total, 0.0)
    out_ref[:HD] = (acc[...] * inverse).astype(BF16)
    write_stats(out_ref, total, top)


def write_stats(out_ref, total, top):
    high = total.astype(BF16).astype(F32)
    row = lax.broadcasted_iota(jnp.int32, (STATS, out_ref.shape[1]), 0)
    stats = jnp.where(row == 0, top, jnp.where(row == 1, high, jnp.where(row == 2, total - high, 0.0)))
    out_ref[HD:] = stats.astype(BF16)


def listed_kernel(blocks, table, *refs):
    q_refs, refs = refs[:blocks], refs[blocks:]
    k_ref, v_ref, refs = refs[0], refs[1], refs[3:]
    out_refs, (stacked, scores, acc) = refs[:blocks], refs[blocks:]
    block_len = k_ref.shape[1]
    columns = stacked.shape[0]
    for j in range(blocks):
        count = table[j, 0]
        stack_heads(q_refs[j], stacked)
        acc[...] = jnp.zeros(acc.shape, F32)

        def first(group, base, i, running):
            at = base + group * i
            keys = jnp.concatenate([k_ref[table[j, 1 + at + g]] for g in range(group)], axis=0)
            found = scores_of(keys, stacked)
            for g in range(group):
                part = found[g * block_len:(g + 1) * block_len]
                if g:
                    part = part + jnp.where(at + g < count, 0.0, NEG).astype(F32)
                scores[at + g] = part
                running = jnp.maximum(running, jnp.max(in_eights(part), axis=0))
            return running

        def second(group, base, i, total):
            at = base + group * i
            found = scores[pl.ds(at, group)].reshape(group * block_len // 8, 8, columns)
            probs = jnp.exp2(found - top_eight[None])
            values = jnp.concatenate([v_ref[table[j, 1 + at + g]] for g in range(group)], axis=0)
            acc[...] += weigh(values, probs.reshape(group * block_len, columns))
            return total + jnp.sum(probs, axis=0)

        def over(step, carry):
            fours = (count + 1) // 4
            carry = lax.fori_loop(0, fours, functools.partial(step, 4, 0), carry)
            rest = (jnp.maximum(count - 4 * fours, 0) + 1) // 2
            return lax.fori_loop(0, rest, functools.partial(step, 2, 4 * fours), carry)

        running = over(first, jnp.full((8, columns), NEG, F32))
        top = jnp.max(running, axis=0, keepdims=True).astype(BF16).astype(F32)
        top_eight = jnp.broadcast_to(top, (8, columns))
        total = jnp.sum(over(second, jnp.zeros((8, columns), F32)), axis=0, keepdims=True)
        write_partial(out_refs[j], acc, total, top)


def attend_listed(after, table, queries, cache_k, cache_v):
    blocks = len(queries)
    tokens, width = queries[0].shape
    columns = tokens * width // HD
    block_len = cache_k.shape[1]
    vmem = pl.BlockSpec(memory_space=pltpu.VMEM)
    keys = blocks * block_len * 6
    return pl.pallas_call(
        functools.partial(listed_kernel, blocks),
        out_shape=[jax.ShapeDtypeStruct((HD + STATS, columns), BF16)] * blocks,
        in_specs=[pl.BlockSpec(memory_space=pltpu.SMEM)] + [vmem] * (blocks + 2) + [pl.BlockSpec(memory_space=pl.ANY)],
        out_specs=[vmem] * blocks,
        scratch_shapes=[
            pltpu.VMEM((columns, 2 * HD), BF16),
            pltpu.VMEM((table.shape[1] - 1, block_len, columns), F32),
            pltpu.VMEM((HD, columns), F32),
        ],
        compiler_params=pltpu.CompilerParams(vmem_limit_bytes=24 * MIB),
        cost_estimate=LIGHT,
    )(table, *queries, cache_k, cache_v, after)


def span_kernel(flag, q_ref, k0, k1, v0, v1, after, out_ref, stacked, acc):
    tokens = q_ref.shape[0]
    stack_heads(q_ref, stacked)
    found = scores_of(jnp.concatenate([k0[...], k1[...]], axis=0), stacked)
    key = lax.broadcasted_iota(jnp.int32, found.shape, 0)
    token = lax.broadcasted_iota(jnp.int32, found.shape, 1) % tokens
    behind = jnp.where(flag[0] > 0, tokens, 0)
    found = jnp.where((key < behind) | ((key >= tokens) & (key - tokens <= token)), found, NEG)
    top = jnp.max(found, axis=0, keepdims=True).astype(BF16).astype(F32)
    probs = jnp.exp2(found - top)
    acc[...] = weigh(jnp.concatenate([v0[...], v1[...]], axis=0), probs)
    write_partial(out_ref, acc, jnp.sum(probs, axis=0, keepdims=True), top)


def attend_span(after, flag, queries, k0, k1, v0, v1):
    tokens, width = queries.shape
    columns = tokens * width // HD
    vmem = pl.BlockSpec(memory_space=pltpu.VMEM)
    return pl.pallas_call(
        span_kernel,
        out_shape=jax.ShapeDtypeStruct((HD + STATS, columns), BF16),
        in_specs=[pl.BlockSpec(memory_space=pltpu.SMEM)] + [vmem] * 5 + [pl.BlockSpec(memory_space=pl.ANY)],
        out_specs=vmem,
        scratch_shapes=[pltpu.VMEM((columns, 2 * HD), BF16), pltpu.VMEM((HD, columns), F32)],
        compiler_params=pltpu.CompilerParams(vmem_limit_bytes=8 * MIB),
        cost_estimate=LIGHT,
    )(flag, queries, k0, k1, v0, v1, after)


def merge_kernel(count, final, *refs):
    parts, out_ref = refs[:count], refs[count + 1]
    stats = [part[HD:].astype(F32) for part in parts]
    tops = [s[0:1] for s in stats]
    top = functools.reduce(jnp.maximum, tops)
    weights = [jnp.exp2(t - top) * (s[1:2] + s[2:3]) for t, s in zip(tops, stats)]
    total = functools.reduce(jnp.add, weights)
    inverse = jnp.where(total > 0, 1.0 / total, 0.0)
    weights = [w * inverse for w in weights]
    tokens = out_ref.shape[0] if final else HD
    for lower in range(0, parts[0].shape[1], tokens):
        columns = slice(lower, lower + tokens)
        joined = functools.reduce(jnp.add, [w[:, columns] * part[:HD, columns].astype(F32) for w, part in zip(weights, parts)])
        if final:
            h = lower // tokens
            out_ref[:, h * HD:(h + 1) * HD] = joined.T.astype(BF16)
        else:
            out_ref[:HD, columns] = joined.astype(BF16)
    if not final:
        write_stats(out_ref, total, top)


def merge(after, parts, tokens=None):
    rows, columns = parts[0].shape
    vmem = pl.BlockSpec(memory_space=pltpu.VMEM)
    shape = (tokens, columns * HD // tokens) if tokens else (rows, columns)
    return pl.pallas_call(
        functools.partial(merge_kernel, len(parts), tokens is not None),
        out_shape=jax.ShapeDtypeStruct(shape, BF16),
        in_specs=[vmem] * len(parts) + [pl.BlockSpec(memory_space=pl.ANY)],
        out_specs=vmem,
        compiler_params=pltpu.CompilerParams(vmem_limit_bytes=8 * MIB),
        cost_estimate=LIGHT,
    )(*parts, after)


def project_kernel(count, picks, has_term, offsets, *refs):
    parts, wo_ref, refs = refs[:count], refs[count], refs[count + 1:]
    term = refs[0] if has_term else None
    out_refs, stacked = refs[has_term + 1:-1], refs[-1]
    tokens = parts[0].shape[0]
    width = out_refs[0].shape[1]
    for k, part in enumerate(parts):
        stacked[k * tokens:(k + 1) * tokens] = part[...]
    for at, j in enumerate(picks):
        start = pl.multiple_of(offsets[j], width)
        found = jnp.dot(stacked[...], wo_ref[:, pl.ds(start, width)], preferred_element_type=F32)
        if has_term:
            found = found + term[:, at * width:(at + 1) * width].astype(F32)
        out_refs[at][...] = found.astype(BF16)


def project(after, offsets, parts, wo, picks, term=None):
    tokens, depth = parts[0].shape
    width = wo.shape[1] // offsets.shape[0]
    rows = len(parts) * tokens
    vmem = pl.BlockSpec(memory_space=pltpu.VMEM)
    terms = [] if term is None else [term]
    return pl.pallas_call(
        functools.partial(project_kernel, len(parts), tuple(picks), len(terms)),
        out_shape=[jax.ShapeDtypeStruct((rows, width), BF16)] * len(picks),
        in_specs=[pl.BlockSpec(memory_space=pltpu.SMEM)] + [vmem] * (len(parts) + 1 + len(terms)) + [pl.BlockSpec(memory_space=pl.ANY)],
        out_specs=[vmem] * len(picks),
        scratch_shapes=[pltpu.VMEM((rows, depth), BF16)],
        compiler_params=pltpu.CompilerParams(vmem_limit_bytes=10 * MIB),
        cost_estimate=LIGHT,
    )(offsets, *parts, wo, *terms, after)


def send_kernel(count, picks, offsets, *refs):
    parts, wo_ref, out_ref, stacked = refs[:count], refs[count], refs[count + 2], refs[count + 3]
    tokens = parts[0].shape[0]
    width = out_ref.shape[1] // len(picks)
    for k, part in enumerate(parts):
        stacked[k * tokens:(k + 1) * tokens] = part[...]
    for at, j in enumerate(picks):
        start = pl.multiple_of(offsets[j], width)
        out_ref[:, at * width:(at + 1) * width] = jnp.dot(
            stacked[...], wo_ref[:, pl.ds(start, width)], preferred_element_type=F32
        ).astype(BF16)


def project_side(after, offsets, parts, wo, picks):
    tokens, depth = parts[0].shape
    rows = len(parts) * tokens
    vmem = pl.BlockSpec(memory_space=pltpu.VMEM)
    return pl.pallas_call(
        functools.partial(send_kernel, len(parts), tuple(picks)),
        out_shape=jax.ShapeDtypeStruct((rows, wo.shape[1] // offsets.shape[0] * len(picks)), BF16),
        in_specs=[pl.BlockSpec(memory_space=pltpu.SMEM)] + [vmem] * (len(parts) + 1) + [pl.BlockSpec(memory_space=pl.ANY)],
        out_specs=vmem,
        scratch_shapes=[pltpu.VMEM((rows, depth), BF16)],
        compiler_params=pltpu.CompilerParams(vmem_limit_bytes=10 * MIB),
        cost_estimate=LIGHT,
    )(offsets, *parts, wo, after)


def add_kernel(splits, one, two, after, *out_refs):
    total = (one[...].astype(F32) + two[...].astype(F32)).astype(BF16)
    rows = total.shape[0] // splits
    for i, out_ref in enumerate(out_refs):
        out_ref[...] = total[i * rows:(i + 1) * rows]


def add(after, one, two, splits):
    rows, width = one.shape
    vmem = pl.BlockSpec(memory_space=pltpu.VMEM)
    return pl.pallas_call(
        functools.partial(add_kernel, splits),
        out_shape=[jax.ShapeDtypeStruct((rows // splits, width), BF16)] * splits,
        in_specs=[vmem] * 2 + [pl.BlockSpec(memory_space=pl.ANY)],
        out_specs=[vmem] * splits,
        compiler_params=pltpu.CompilerParams(vmem_limit_bytes=8 * MIB),
        cost_estimate=LIGHT,
    )(one, two, after)


def join_kernel(after, *refs):
    sources, out_ref = refs[:-1], refs[-1]
    rows = sources[0].shape[0]
    for i, source in enumerate(sources):
        out_ref[i * rows:(i + 1) * rows] = source[...]


def join(after, sources):
    rows, width = sources[0].shape
    vmem = pl.BlockSpec(memory_space=pltpu.VMEM)
    return pl.pallas_call(
        join_kernel,
        out_shape=jax.ShapeDtypeStruct((len(sources) * rows, width), BF16),
        in_specs=[pl.BlockSpec(memory_space=pl.ANY)] + [vmem] * len(sources),
        out_specs=vmem,
        compiler_params=pltpu.CompilerParams(vmem_limit_bytes=8 * MIB),
        cost_estimate=LIGHT,
    )(after, *sources)


def place_kernel(blocks, chunk, tokens, offsets, *refs):
    out_ref, sem = refs[-2:]
    copies = []
    for ref, at, j, k in blocks:
        width = refs[ref].shape[1]
        start = pl.multiple_of(offsets[j, k], width)
        copies.append(pltpu.make_async_copy(
            refs[ref].at[pl.ds(at * tokens, tokens)],
            out_ref.at[pl.ds(chunk * tokens, tokens), pl.ds(start, width)],
            sem.at[len(copies)],
        ))
    for copy in copies:
        copy.start()
    for copy in copies:
        copy.wait()


def place(after, offsets, arrays, blocks, chunk, tokens, shape, before):
    vmem = pl.BlockSpec(memory_space=pltpu.VMEM)
    hbm = pl.BlockSpec(memory_space=pl.ANY)
    held = [] if before is None else [before]
    return pl.pallas_call(
        functools.partial(place_kernel, tuple(blocks), chunk, tokens),
        out_shape=jax.ShapeDtypeStruct(shape, BF16),
        in_specs=[pl.BlockSpec(memory_space=pltpu.SMEM)] + [vmem] * len(arrays) + [hbm] * (1 + len(held)),
        out_specs=hbm,
        scratch_shapes=[pltpu.SemaphoreType.DMA((len(blocks),))],
        input_output_aliases={1 + len(arrays): 0} if held else {},
        compiler_params=pltpu.CompilerParams(vmem_limit_bytes=8 * MIB),
        cost_estimate=LIGHT,
    )(offsets, *arrays, *held, after)


def body(queries, span_k, span_v, cache_k, cache_v, block_slot, pattern, wo):
    n_z, n_x, n_h = (lax.axis_size(a) for a in ("fsdp", "seq", "head"))
    z, x, me = (lax.axis_index(a) for a in ("fsdp", "seq", "head"))
    chunks, list_len = pattern.shape
    cb_local, block_len, _ = cache_k.shape
    index_here = z * n_x + x
    capacity = min(max(2, 2 * chunks * list_len // (n_z * n_x)), list_len)
    capacity = -(-capacity // 4) * 4

    slots = block_slot[pattern]
    slots = jnp.stack([slots] + [swap(slots, "fsdp", k) for k in range(1, n_z)])
    slots = jnp.stack([slots] + [swap(slots, "seq", s) for s in range(1, n_x)])
    within = slots - index_here * cb_local
    mine = (within >= 0) & (within < cb_local)
    before = jnp.tri(list_len, list_len, -1, dtype=bool)
    rank = jnp.sum((mine[..., None, :] & before).astype(jnp.int32), axis=-1)
    rank = jnp.where(mine, rank, -1)
    chosen = rank[..., None, :] == jnp.arange(capacity)[:, None]
    compact = jnp.sum(jnp.where(chosen, within[..., None, :], 0), axis=-1)
    table = jnp.concatenate([jnp.sum(mine.astype(jnp.int32), axis=-1, keepdims=True), compact], axis=-1)

    prior = lax.ppermute(
        jnp.concatenate([span_k[-block_len:], span_v[-block_len:]], axis=1),
        ("fsdp", "seq"), [(i, i + 1) for i in range(n_z * n_x - 1)],
    )

    quarter = wo.shape[1] // n_h
    picked = jnp.stack([(me ^ j) * quarter for j in range(n_h)])
    offsets = jnp.stack([jnp.stack([(z ^ k) * wo.shape[1] + (me ^ j) * quarter for k in range(n_z)]) for j in range(n_h)])

    last = [queries]

    def run(call, *args):
        result = call(last[0], *args)
        if call is not place:
            last[0] = result[0] if isinstance(result, (list, tuple)) else result
        return result

    far_first = []
    distance = n_z
    while distance > 1:
        distance //= 2
        far_first.append(distance)
    blocks_of = [slice(c * block_len, (c + 1) * block_len) for c in range(chunks)]

    def over_z(block):
        held = {0: block}
        for distance in far_first:
            for k in list(held):
                held[k ^ distance] = swap(held[k], "fsdp", distance)
        return held

    by_z, gathered, span_parts = [], [], []
    for c in range(chunks):
        by_z.append(over_z(queries[blocks_of[c]]))
        gathered.append({(s, k): swap(q, "seq", s) for k, q in by_z[c].items() for s in range(1, n_x)})
    for c in range(chunks):
        if c == 0:
            k0, v0 = prior[:, :HD], prior[:, HD:]
        else:
            k0, v0 = span_k[blocks_of[c - 1]], span_v[blocks_of[c - 1]]
        flag = (index_here * chunks + c > 0).astype(jnp.int32).reshape(1)
        span_parts.append(run(attend_span, flag, by_z[c][0], k0, span_k[blocks_of[c]], v0, span_v[blocks_of[c]]))

    near = [k for k in range(n_z) if k % 2] or [0]
    rest = [k for k in range(n_z) if k % 2 == 0 and k not in near]
    parts = [{k: [] for k in range(n_z)} for _ in range(chunks)]

    def listed(c, s, ks):
        if not ks:
            return
        queries_of = [by_z[c][k] if s == 0 else gathered[c][s, k] for k in ks]
        rows = jnp.stack([table[s, k, c] for k in ks])
        found = run(attend_listed, rows, queries_of, cache_k, cache_v)
        for k, part in zip(ks, found):
            parts[c][k].append(part if s == 0 else swap(part, "seq", s))

    def away(c, ks):
        for s in range(1, n_x):
            listed(c, s, ks)

    def here(c, ks):
        listed(c, 0, ks)

    def pass_on(c, distance):
        for k in range(n_z):
            if k & distance and k % distance == 0:
                parts[c][k ^ distance].append(swap(run(merge, parts[c][k]), "fsdp", distance))

    def merge_to(c, k, distance):
        parts[c][k ^ distance].append(swap(run(merge, parts[c][k]), "fsdp", distance))

    attended = {}

    def attend(c):
        attended[c] = over_z(run(merge, parts[c][0] + [span_parts[c]], block_len))

    even = [j for j in range(n_h) if j % 2 == 0]
    odd = [j ^ 1 for j in even]
    state = {}
    shape = (chunks * block_len, n_z * wo.shape[1])

    def project_sent(c, ks):
        rows_of = [attended[c][k] for k in ks]
        state[c, ks[0]] = swap(run(project_side, picked, rows_of, wo, odd), "head", 1)

    def project_kept(c, ks):
        rows_of = [attended[c][k] for k in ks]
        held = dict(zip(even, run(project, picked, rows_of, wo, even, state[c, ks[0]])))
        state[c, ks[0]] = (held[0], swap(held[2], "head", 2))

    def total(c, ks):
        rows_of = run(add, *state[c, ks[0]], len(ks))
        state[c, ks[0]] = [swap(r, "fsdp", k) if k else r for k, r in zip(ks, rows_of)]

    def spread(c, ks):
        first = run(join, state[c, ks[0]])
        state[c, ks[0]] = [first, swap(first, "head", 2)]

    def spread_on(c, ks):
        both = run(join, state[c, ks[0]])
        state[c, ks[0]] = [both, swap(both, "head", 1)]

    mixed = [None]

    def put(c, ks):
        blocks = [
            (ref, at * len(ks) + i, j, k)
            for ref, columns in enumerate((even, odd)) for at, j in enumerate(columns) for i, k in enumerate(ks)
        ]
        mixed[0] = run(place, offsets, state[c, ks[0]], blocks, c, block_len, shape, mixed[0])

    low, high, whole = list(range(n_z // 2)), list(range(n_z // 2, n_z)), list(range(n_z))
    assert chunks == 2 and n_z == 4 and n_h == 4
    A, B = 0, 1
    away(A, rest)
    away(A, near)
    here(A, near)
    here(A, rest)
    merge_to(A, 1, 1)
    merge_to(A, 3, 1)
    away(B, rest)
    merge_to(A, 2, 2)
    away(B, near)
    here(B, near)
    attend(A)
    merge_to(B, 1, 1)
    merge_to(B, 3, 1)
    here(B, rest)
    merge_to(B, 2, 2)
    project_sent(A, whole)
    project_kept(A, whole)
    attend(B)
    total(A, whole)
    project_sent(B, whole)
    project_kept(B, whole)
    spread(A, whole)
    total(B, whole)
    spread_on(A, whole)
    spread(B, whole)
    put(A, whole)
    spread_on(B, whole)
    put(B, whole)
    return mixed[0]


def solution(mesh):
    return jax.shard_map(
        body,
        mesh=mesh,
        in_specs=(
            P(("fsdp", "seq"), "head"),
            P(("fsdp", "seq"), "head"),
            P(("fsdp", "seq"), "head"),
            P(("fsdp", "seq"), None, "head"),
            P(("fsdp", "seq"), None, "head"),
            P(),
            P(("fsdp", "seq"), None),
            P("head", "fsdp"),
        ),
        out_specs=P(("fsdp", "seq"), None),
        check_vma=False,
    )
```
